512 devices in a mesh: leaf: 128 (over y, z, core), sub: 4 (over x).
Axes of the slice: x: 4, y: 8, z: 8, core: 2. Of those that a mesh axis runs over, the one named last changes fastest.
Arguments:
- points: float32 [524288, 64], P(('leaf', 'sub')), may hold values from -6 to 6
- charges: float32 [524288, 16], P(('leaf', 'sub')), may hold values from -4.5 to 5.5
- order: int32 [512, 1024], P(('leaf', 'sub')), may hold values from 0 to 1023, each once within a row
- neighbours: int32 [1024, 32], P(('leaf', 'sub')), may hold values from 0 to 1023, as said below
- neighbour_mask: int32 [1024, 32], P(('leaf', 'sub')), may hold values from 0 to 1, as said below
- leaf_skel: int32 [1024, 128], P(('leaf', 'sub')), may hold values from 0 to 511, as said below
- pair_skel: int32 [512, 128], P(('leaf', 'sub')), may hold values from 0 to 255, as said below
- upper_skel: int32 [512, 128], replicated, may hold values from 0 to 255, as said below
Outputs:
- potentials: float32 [524288, 16], P(('leaf', 'sub'))
The draws below stay inside these ranges and needn't reach their ends.
Inputs may be any that keep to these rules, and one draw needn't show every extreme that they name: `order`: each row is a permutation of the rows of one device's block. `neighbours`: for a leaf of group g (leaves g * 8 to (g + 1) * 8 - 1), the live slots name distinct leaves of groups g - 1, g and g + 1; a padded slot names the leaf itself. `neighbour_mask`: at most 24 live slots in a list. `leaf_skel`: distinct entries in a row. `pair_skel`: distinct entries in a row. `upper_skel`: distinct entries in a row; rows 0 and 1 are not read.
All inputs are finite; a program needn't handle non-finite values.
Results may differ from the reference program's by a relative error of at most 0.0034.
Values may be sent and summed in bfloat16 or wider, within the bound.
A program may use at most 128 MiB of HBM per device.

```python
import math
import jax
import jax.numpy as jnp
from jax import lax

DIM = 64
SKEL = 128
LEAF = 512
RHS = 16
NBR = 32
GRP = 8
LEAVES = 1024
PTS_DEV = 1024
POINTS = 524288
N_LEAF = 128
N_SUB = 4


def near_lists(key):
    key_live, key_perm = jax.random.split(key)
    leaf_ids = jnp.arange(LEAVES, dtype=jnp.int32)
    group_ids = leaf_ids // GRP
    live_count = jax.random.randint(key_live, (LEAVES,), 4, 3 * GRP + 1).astype(jnp.int32)
    live_count = jnp.where(leaf_ids % (2 * GRP) == GRP + 1, 3 * GRP, live_count)
    orders = jax.vmap(lambda subkey: jax.random.permutation(subkey, 3 * GRP))(jax.random.split(key_perm, LEAVES))
    candidate = (group_ids[:, None] - 1) * GRP + orders.astype(jnp.int32)
    slot_ids = jnp.arange(3 * GRP, dtype=jnp.int32)
    valid = (slot_ids[None, :] < live_count[:, None]) & (candidate >= 0) & (candidate < LEAVES)
    chosen = jnp.where(valid, candidate, leaf_ids[:, None])
    padding = jnp.broadcast_to(leaf_ids[:, None], (LEAVES, NBR - 3 * GRP))
    listed = jnp.concatenate([chosen, padding], axis=1).astype(jnp.int32)
    masked = jnp.concatenate([valid.astype(jnp.int32), jnp.zeros((LEAVES, NBR - 3 * GRP), jnp.int32)], axis=1)
    return (listed, masked)


def first_rows(key, row_count, total):
    keys = jax.random.split(key, row_count)
    return jax.vmap(lambda subkey: jax.random.permutation(subkey, total)[:SKEL])(keys).astype(jnp.int32)


def draw_points(key, part):
    key = jax.random.fold_in(key, 21)
    spread = math.sqrt(DIM / 8.0 * ((5.0 * SKEL) ** (2.0 / DIM) - 1.0))
    values = jnp.clip(spread * jax.random.normal(key, (POINTS, DIM), jnp.float32), -6.0, 6.0)
    return values


def draw_charges(key, part):
    key = jax.random.fold_in(key, 22)
    key_noise = jax.random.fold_in(key, 0)
    values = 0.5 + jnp.clip(jax.random.normal(key_noise, (POINTS, RHS), jnp.float32), -5.0, 5.0)
    return values


def draw_neighbours(key, part):
    return near_lists(key)[0]


def draw_neighbour_mask(key, part):
    return near_lists(key)[1]


def draw_leaf_skel(key, part):
    key = jax.random.fold_in(key, 11)
    return first_rows(key, LEAVES, LEAF)


def draw_pair_skel(key, part):
    key = jax.random.fold_in(key, 12)
    return first_rows(key, N_LEAF * N_SUB, 2 * SKEL)


def draw_upper_skel(key, part):
    key = jax.random.fold_in(key, 13)
    return first_rows(key, N_LEAF * N_SUB, 2 * SKEL)


def setup_inputs(seed: int = 0) -> dict:
    splits = jax.random.split(jax.random.key(seed), 9)
    points = draw_points(jax.random.fold_in(splits[8], 71), 0)
    charges = draw_charges(jax.random.fold_in(splits[8], 71), 0)
    order = jax.vmap(lambda own: jax.random.permutation(own, PTS_DEV))(jax.random.split(splits[2], (N_LEAF * N_SUB))).reshape((N_LEAF * N_SUB, PTS_DEV)).astype(jnp.int32)
    neighbours = draw_neighbours(jax.random.fold_in(splits[8], 71), 0)
    neighbour_mask = draw_neighbour_mask(jax.random.fold_in(splits[8], 71), 0)
    leaf_skel = draw_leaf_skel(jax.random.fold_in(splits[8], 71), 0)
    pair_skel = draw_pair_skel(jax.random.fold_in(splits[8], 71), 0)
    upper_skel = draw_upper_skel(jax.random.fold_in(splits[8], 71), 0)
    return dict(points=points, charges=charges, order=order, neighbours=neighbours, neighbour_mask=neighbour_mask, leaf_skel=leaf_skel, pair_skel=pair_skel, upper_skel=upper_skel)


highest = lax.Precision.HIGHEST


def kernel(left_pts, right_pts):
    left_sq = jnp.sum(jnp.square(left_pts.astype(jnp.float32)), axis=-1)
    right_sq = jnp.sum(jnp.square(right_pts.astype(jnp.float32)), axis=-1)
    inner = jnp.dot(left_pts, right_pts.T, preferred_element_type=jnp.float32)
    return jnp.exp((-2.0 / left_pts.shape[-1]) * (left_sq[:, None] + right_sq[None, :] - 2.0 * inner))


def pair_far(node_pts, node_up):
    pair_pts = node_pts.reshape(-1, 2, SKEL, DIM)
    pair_up = node_up.reshape(-1, 2, SKEL, RHS)
    cross_mat = jax.vmap(kernel)(pair_pts[:, 0], pair_pts[:, 1])
    to_left = jnp.einsum("nab,nbr->nar", cross_mat, pair_up[:, 1], precision=highest)
    to_right = jnp.einsum("nab,nar->nbr", cross_mat, pair_up[:, 0], precision=highest)
    return jnp.stack([to_left, to_right], axis=1).reshape(-1, SKEL, RHS)


def reference(points, charges, order, neighbours, neighbour_mask, leaf_skel, pair_skel, upper_skel):
    blocks = N_LEAF * N_SUB
    tree_pts = jnp.take_along_axis(points.reshape(blocks, PTS_DEV, DIM), order[:, :, None], axis=1)
    tree_chg = jnp.take_along_axis(charges.reshape(blocks, PTS_DEV, RHS), order[:, :, None], axis=1)
    leaf_pts = tree_pts.reshape(LEAVES, LEAF, DIM).astype(jnp.bfloat16)
    leaf_chg = tree_chg.reshape(LEAVES, LEAF, RHS)
    leaf_low = leaf_chg.astype(jnp.bfloat16)

    def near_leaf(item):
        own_pts, leaf_ids, live_mask = item

        def add_slot(slot_number, running):
            other = leaf_ids[slot_number]
            weights = kernel(own_pts, leaf_pts[other]).astype(jnp.bfloat16)
            contrib = jnp.dot(weights, leaf_low[other], preferred_element_type=jnp.float32)
            return running + live_mask[slot_number].astype(jnp.float32) * contrib

        return lax.fori_loop(0, NBR, add_slot, jnp.zeros((LEAF, RHS), jnp.float32))

    near_field = lax.map(near_leaf, (leaf_pts, neighbours, neighbour_mask))
    skel_pts = jnp.take_along_axis(leaf_pts, leaf_skel[:, :, None], axis=1)

    def leaf_up(item):
        skel_rows, own_pts, own_chg = item
        return jnp.dot(kernel(skel_rows, own_pts), own_chg, precision=highest)

    node_up = lax.map(leaf_up, (skel_pts, leaf_pts, leaf_chg))
    tree_depth = LEAVES.bit_length() - 1
    node_sets = [skel_pts]
    node_ups = [node_up]
    parent_mats = [None]
    for tree_level in range(1, tree_depth):
        children = node_sets[-1].reshape(-1, 2 * SKEL, DIM)
        child_up = node_ups[-1].reshape(-1, 2 * SKEL, RHS)
        if tree_level == 1:
            chosen = pair_skel
        else:
            node_count = LEAVES >> tree_level
            chosen = upper_skel[node_count:2 * node_count]
        parent_pts = jnp.take_along_axis(children, chosen[:, :, None], axis=1)
        parent_mat = jax.vmap(kernel)(parent_pts, children)
        node_sets.append(parent_pts)
        node_ups.append(jnp.einsum("nsc,ncr->nsr", parent_mat, child_up, precision=highest))
        parent_mats.append(parent_mat)
    far_terms = [pair_far(node_sets[tree_level], node_ups[tree_level]) for tree_level in range(tree_depth)]
    down_term = far_terms[tree_depth - 1]
    for tree_level in range(tree_depth - 1, 0, -1):
        back_term = jnp.einsum("nsc,nsr->ncr", parent_mats[tree_level], down_term, precision=highest)
        down_term = far_terms[tree_level - 1] + back_term.reshape(-1, SKEL, RHS)

    def leaf_down(item):
        skel_rows, own_pts, leaf_term = item
        return jnp.dot(kernel(skel_rows, own_pts).T, leaf_term, precision=highest)

    far_field = lax.map(leaf_down, (skel_pts, leaf_pts, down_term))
    tree_out = (near_field + far_field).reshape(blocks, PTS_DEV, RHS)
    placed = jax.vmap(lambda values, target: jnp.zeros_like(values).at[target].set(values))(tree_out, order)
    return placed.reshape(POINTS, RHS)
```

```python
import functools

import jax
import jax.numpy as jnp
from jax import lax
from jax.experimental import pallas as pl
from jax.experimental.pallas import tpu as pltpu
from jax.sharding import PartitionSpec as P

F32 = jnp.float32
BF16 = jnp.bfloat16
MESH = pl.DeviceIdType.MESH
TN = (((0,), (0,)), ((), ()))
NT = (((1,), (1,)), ((), ()))
LOG2E = 1.4426950408889634

DIM = 64
AUG = 16
RHS = 16
PTS = 1024
SKEL = 128
HALF = PTS // 2
AUGD = DIM + AUG
WROWS = AUGD + RHS
NROWS = AUGD + 2 * RHS


def split2(value):
    high = value.astype(BF16)
    return high, (value - high.astype(F32)).astype(BF16)


def split3(value):
    high = value.astype(BF16)
    rest = value - high.astype(F32)
    mid = rest.astype(BF16)
    return high.astype(F32), mid.astype(F32), (rest - mid.astype(F32)).astype(BF16).astype(F32)


def augment(pts_f32, member):
    width = pts_f32.shape[1]
    n = -0.5 * jnp.sum(pts_f32 * pts_f32, axis=0, keepdims=True)
    hi, mid, lo = split3(n)
    row = lax.broadcasted_iota(jnp.int32, (AUG, width), 0)
    out = jnp.where(row == 0, hi, jnp.where(row == 1, mid, jnp.where(row == 2, lo, 0.0)))
    out = jnp.where(row == 3, member, out)
    return jnp.where((row >= 8) & (row < 11), 1.0, out)


def swapped(block):
    aug = block[DIM:AUGD].astype(F32)
    aug = jnp.concatenate([aug[8:], aug[:8]], axis=0).astype(BF16)
    return jnp.concatenate([block[:DIM], aug], axis=0)


def gauss(std, swp):
    scale = LOG2E * 4.0 / DIM
    inner = lax.dot_general(std, swp, TN, preferred_element_type=F32)
    return jnp.exp2(inner * scale)


def apply_mat(u_hi, u_lo, mat):
    k_hi, k_lo = split2(mat)
    n = u_hi.shape[0]
    both = jnp.dot(jnp.concatenate([u_hi, u_lo], axis=0), k_hi, preferred_element_type=F32)
    return both[:n] + both[n:] + jnp.dot(u_hi, k_lo, preferred_element_type=F32)


def onehot(sel, rows):
    at = lax.broadcasted_iota(jnp.int32, (rows, sel.shape[1]), 0)
    return jnp.where(at == sel, 1.0, 0.0).astype(BF16)


def body(
    y_size, z_size,
    pts_ref, chg_ref, order_ref, nbr_ref, msk_ref, lsk_ref, psk_ref, usk_ref,
    out_ref,
    win, own_swp, acc, cnt, tree, lvl4, lvl2, leaf_nodes, far, downs,
    wsend, wrecv, tsend, trecv,
):
    leaf = lax.axis_index("leaf")
    sub = lax.axis_index("sub")
    leaf_count = lax.axis_size("leaf")
    device = leaf * 4 + sub
    core = leaf % 2
    z = (leaf // 2) % z_size
    y = leaf // (2 * z_size)
    prev = (leaf + leaf_count - 1) % leaf_count
    nxt = (leaf + 1) % leaf_count
    partner = leaf + 1 - 2 * core

    def x_peer(step):
        return (leaf, (sub + step) % 4)

    def z_peer(step):
        return ((y * z_size + (z + step) % z_size) * 2 + core, sub)

    def y_peer(step):
        return ((((y + step) % y_size) * z_size + z) * 2 + core, sub)

    other_core = [(partner, (sub + step) % 4) for step in range(4)]
    beyond = (leaf + leaf_count - 1 + 2 * core) % leaf_count
    greet = [x_peer(s) for s in (1, 2, 3)] + other_core + [(beyond, sub)]
    greet += [z_peer(s) for s in range(1, z_size)] + [y_peer(s) for s in range(1, y_size)]
    barrier = pltpu.get_barrier_semaphore()
    for peer in greet:
        pl.semaphore_signal(barrier, inc=1, device_id=peer, device_id_type=MESH)

    order = order_ref[...]
    second = order[:, HALF:]
    hi_hot = onehot(second // 128, 8)
    lo_hot = onehot(second % 128, 128)
    grid = lax.dot_general(hi_hot, lo_hot, NT, preferred_element_type=F32)
    member = jnp.concatenate([grid[k : k + 1] for k in range(8)], axis=1)

    pts = pts_ref[...].astype(BF16)
    chg = chg_ref[...]
    chg_hi, chg_lo = split2(chg)
    win[4, 0:DIM] = pts
    win[4, DIM:AUGD] = augment(pts.astype(F32), member).astype(BF16)
    win[4, AUGD:WROWS] = chg_hi

    pl.semaphore_wait(barrier, len(greet))

    def window_copy(slot, target_slot, index, peer):
        return pltpu.make_async_remote_copy(
            src_ref=win.at[slot], dst_ref=win.at[target_slot],
            send_sem=wsend.at[index], recv_sem=wrecv.at[target_slot],
            device_id=peer, device_id_type=MESH,
        )

    sends = []
    for step in (1, 3, 2):
        sends.append(window_copy(4, 4 + (4 - step) % 4, step - 1, x_peer(step)))
    sends.append(window_copy(4, 8, 3, (prev, sub)))
    sends.append(window_copy(4, 0, 4, (nxt, sub)))
    for copy in sends:
        copy.start()

    def window_wait(slot):
        pltpu.make_async_copy(win.at[slot], win.at[slot], wrecv.at[slot]).wait()

    k = lax.broadcasted_iota(jnp.int32, (24, 32), 0)
    slot_k = k // 2
    ids = ((leaf + slot_k // 4 - 1) * 4 + (sub + slot_k % 4) % 4) * 2 + k % 2
    for own in range(2):
        hit = jnp.where(nbr_ref[own : own + 1, :] == ids, msk_ref[own : own + 1, :], 0)
        total = jnp.sum(hit.astype(F32), axis=1, keepdims=True)
        cnt[own] = jnp.broadcast_to(total, (24, 128))

    own_block = win[4, 0:AUGD]
    own_swp[...] = swapped(own_block)
    coarse = (order // 32).astype(F32)
    fine = (order % 32).astype(F32)
    for own in range(2):
        pick = onehot(lsk_ref[own : own + 1, :], HALF)
        part = slice(own * HALF, (own + 1) * HALF)
        place = jnp.concatenate([coarse[:, part], fine[:, part]], axis=0)
        place = jnp.concatenate([place, jnp.zeros((6, HALF), F32)], axis=0).astype(BF16)
        found = jnp.dot(place, pick, preferred_element_type=F32)
        where = (found[0:1] * 32.0 + found[1:2]).astype(jnp.int32)
        skel = jnp.dot(own_block, onehot(where, PTS), preferred_element_type=F32).astype(BF16)
        mine = member if own else 1.0 - member
        mat = gauss(own_block, swapped(skel))
        weights = apply_mat(
            (chg_hi.astype(F32) * mine).astype(BF16), (chg_lo.astype(F32) * mine).astype(BF16), mat
        )
        leaf_nodes[own, 0:AUGD] = skel
        u_hi, u_lo = split2(weights)
        leaf_nodes[own, AUGD : AUGD + RHS] = u_hi
        leaf_nodes[own, AUGD + RHS : NROWS] = u_lo

    def parent_of(left, right, sel):
        both = jnp.concatenate([left, right], axis=1)
        children = both[0:AUGD]
        chosen = jnp.dot(children, onehot(sel, 2 * SKEL), preferred_element_type=F32).astype(BF16)
        mat = gauss(children, swapped(chosen))
        u_hi, u_lo = split2(apply_mat(both[AUGD : AUGD + RHS], both[AUGD + RHS : NROWS], mat))
        return jnp.concatenate([chosen, u_hi, u_lo], axis=0)

    def cross(mine, other):
        mat = gauss(other[0:AUGD], swapped(mine))
        return apply_mat(other[AUGD : AUGD + RHS], other[AUGD + RHS : NROWS], mat)

    def down_mat(index, parent, child):
        k_hi, k_lo = split2(gauss(parent[0:AUGD], swapped(child)))
        downs[index, 0] = k_hi
        downs[index, 1] = k_lo

    def down(index, value):
        v_hi, v_lo = split2(value)
        both = jnp.dot(
            jnp.concatenate([v_hi, v_lo], axis=0), downs[index, 0], preferred_element_type=F32
        )
        return both[:RHS] + both[RHS:] + jnp.dot(v_hi, downs[index, 1], preferred_element_type=F32)

    place8 = [core * 4 + sub, z, y]
    tree[0, pl.ds(place8[0], 1)] = parent_of(leaf_nodes[0], leaf_nodes[1], psk_ref[...])[None]

    def tree_copies(stage):
        slot = place8[stage]
        if stage == 0:
            peers = [x_peer(s) for s in (1, 3, 2)] + other_core
        elif stage == 1:
            peers = [z_peer(s) for s in range(1, z_size)]
        else:
            peers = [y_peer(s) for s in range(1, y_size)]
        return [
            pltpu.make_async_remote_copy(
                src_ref=tree.at[stage, slot], dst_ref=tree.at[stage, slot],
                send_sem=tsend.at[stage, i], recv_sem=trecv.at[stage, slot],
                device_id=peer, device_id_type=MESH,
            )
            for i, peer in enumerate(peers)
        ]

    def tree_wait(stage):
        def one(step, carry):
            slot = (place8[stage] + step) % 8
            pltpu.make_async_copy(
                tree.at[stage, slot], tree.at[stage, slot], trecv.at[stage, slot]
            ).wait()
            return carry

        lax.fori_loop(1, 8, one, 0)

    tree_sends = [tree_copies(0)]
    for copy in tree_sends[0]:
        copy.start()

    relays = []
    for i, dx in enumerate((1, 3, 2)):
        window_wait(4 + dx)
        relays.append(window_copy(4 + dx, 8 + dx, 5 + 2 * i, (prev, sub)))
        relays.append(window_copy(4 + dx, dx, 6 + 2 * i, (nxt, sub)))
        relays[-2].start()
        relays[-1].start()

    acc[...] = jnp.zeros_like(acc)

    def near(slot):
        aug = win[slot, DIM:AUGD].astype(F32)
        group = aug[3:4]
        charge = win[slot, AUGD:WROWS].astype(F32)
        rows = []
        for own in range(2):
            c0 = cnt[own, pl.ds(2 * slot, 1), 0:1]
            c1 = cnt[own, pl.ds(2 * slot + 1, 1), 0:1]
            rows.append(charge * (c0 + (c1 - c0) * group))
        rows = jnp.concatenate(rows, axis=0).astype(BF16)
        mat = gauss(win[slot, 0:AUGD], own_swp[...]).astype(BF16)
        acc[...] += jnp.dot(rows, mat, preferred_element_type=F32)

    def level(stage):
        counts = {0: (256, 128, 64), 1: (32, 16, 8), 2: (4, 2, 0)}[stage]
        base = {0: device // 8, 1: device // 64, 2: 0 * device}[stage]
        me = place8[stage]
        for j in range(4):
            sel = usk_ref[pl.ds(counts[0] + base * 4 + j, 1), :]
            lvl4[stage, j] = parent_of(tree[stage, 2 * j], tree[stage, 2 * j + 1], sel)
        for j in range(2):
            sel = usk_ref[pl.ds(counts[1] + base * 2 + j, 1), :]
            lvl2[stage, j] = parent_of(lvl4[stage, 2 * j], lvl4[stage, 2 * j + 1], sel)
        if stage < 2:
            sel = usk_ref[pl.ds(counts[2] + base, 1), :]
            top = parent_of(lvl2[stage, 0], lvl2[stage, 1], sel)
            tree[stage + 1, pl.ds(place8[stage + 1], 1)] = top[None]
            tree_sends.append(tree_copies(stage + 1))
            for copy in tree_sends[-1]:
                copy.start()

    def path(stage):
        me = place8[stage]
        a, b, c = me, me // 2, me // 4
        node8, sib8 = tree[stage, a], tree[stage, a + 1 - 2 * (a % 2)]
        node4, sib4 = lvl4[stage, b], lvl4[stage, b + 1 - 2 * (b % 2)]
        node2, sib2 = lvl2[stage, c], lvl2[stage, 1 - c]
        far[3 * stage] = cross(node8, sib8)
        far[3 * stage + 1] = cross(node4, sib4)
        far[3 * stage + 2] = cross(node2, sib2)
        down_mat(3 * stage, node4, node8)
        down_mat(3 * stage + 1, node2, node4)
        if stage < 2:
            down_mat(3 * stage + 2, tree[stage + 1, place8[stage + 1]], node2)

    near(4)

    def group_block(i, carry):
        near(4 + i)
        return carry

    def side_block(i, carry):
        dx = (i // 2) + (i // 4) * (1 - 2 * ((i // 2) % 2))
        slot = dx + 8 * (i % 2)
        window_wait(slot)
        near(slot)
        return carry

    lax.fori_loop(1, 4, group_block, 0)
    tree_wait(0)
    level(0)
    path(0)
    lax.fori_loop(0, 4, side_block, 0)
    tree_wait(1)
    level(1)
    path(1)
    lax.fori_loop(4, 8, side_block, 0)
    tree_wait(2)
    level(2)
    path(2)

    value = far[8]
    for index in range(7, -1, -1):
        value = far[index] + down(index, value)
    node = tree[0, place8[0]]
    v_hi, v_lo = split2(value)
    for own in range(2):
        mat = gauss(node[0:AUGD], swapped(leaf_nodes[own]))
        term = cross(leaf_nodes[own], leaf_nodes[1 - own]) + apply_mat(v_hi, v_lo, mat)
        t_hi, t_lo = split2(term)
        mat = gauss(leaf_nodes[own, 0:AUGD], own_swp[...])
        acc[own * RHS : (own + 1) * RHS] += apply_mat(t_hi, t_lo, mat)

    mine = win[4, DIM:AUGD].astype(F32)[3:4]
    out_ref[...] = jnp.where(mine > 0.5, acc[RHS:], acc[:RHS])

    for copy in sends + relays:
        copy.wait_send()
    for group in tree_sends:
        for copy in group:
            copy.wait_send()


def shards(points, charges, order, neighbours, neighbour_mask, leaf_skel, pair_skel, upper_skel):
    call = pl.pallas_call(
        functools.partial(body, 8, 8),
        out_shape=jax.ShapeDtypeStruct((RHS, PTS), F32),
        in_specs=[pl.BlockSpec(memory_space=pltpu.VMEM)] * 8,
        out_specs=pl.BlockSpec(memory_space=pltpu.VMEM),
        scratch_shapes=[
            pltpu.VMEM((12, WROWS, PTS), BF16),
            pltpu.VMEM((AUGD, PTS), BF16),
            pltpu.VMEM((2 * RHS, PTS), F32),
            pltpu.VMEM((2, 24, 128), F32),
            pltpu.VMEM((3, 8, NROWS, SKEL), BF16),
            pltpu.VMEM((3, 4, NROWS, SKEL), BF16),
            pltpu.VMEM((3, 2, NROWS, SKEL), BF16),
            pltpu.VMEM((2, NROWS, SKEL), BF16),
            pltpu.VMEM((9, RHS, SKEL), F32),
            pltpu.VMEM((8, 2, SKEL, SKEL), BF16),
            pltpu.SemaphoreType.DMA((11,)),
            pltpu.SemaphoreType.DMA((12,)),
            pltpu.SemaphoreType.DMA((3, 7)),
            pltpu.SemaphoreType.DMA((3, 8)),
        ],
        compiler_params=pltpu.CompilerParams(
            collective_id=0, has_side_effects=True, vmem_limit_bytes=56 << 20
        ),
        name="krr_matvec",
    )
    out = call(
        points.T, charges.T, order, neighbours, neighbour_mask, leaf_skel, pair_skel, upper_skel
    )
    return out.T


def solution(mesh):
    placed = (P(("leaf", "sub"), None),) * 7 + (P(),)
    return jax.shard_map(
        shards, mesh=mesh, in_specs=placed, out_specs=P(("leaf", "sub"), None), check_vma=False
    )
```

```python
import functools

import jax
import jax.numpy as jnp
from jax import lax
from jax.experimental import pallas as pl
from jax.experimental.pallas import tpu as pltpu
from jax.sharding import PartitionSpec as P

F32 = jnp.float32
BF16 = jnp.bfloat16
MESH = pl.DeviceIdType.MESH
TN = (((0,), (0,)), ((), ()))
NT = (((1,), (1,)), ((), ()))
LOG2E = 1.4426950408889634

DIM = 64
AUG = 16
RHS = 16
PTS = 1024
SKEL = 128
HALF = PTS // 2
AUGD = DIM + AUG
WROWS = AUGD + RHS
UROWS = 2 * RHS


def split2(value):
    high = value.astype(BF16)
    return high, (value - high.astype(F32)).astype(BF16)


def split3(value):
    high = value.astype(BF16)
    rest = value - high.astype(F32)
    mid = rest.astype(BF16)
    return high.astype(F32), mid.astype(F32), (rest - mid.astype(F32)).astype(BF16).astype(F32)


def augment(pts_f32, member):
    width = pts_f32.shape[1]
    n = -0.5 * jnp.sum(pts_f32 * pts_f32, axis=0, keepdims=True)
    hi, mid, lo = split3(n)
    row = lax.broadcasted_iota(jnp.int32, (AUG, width), 0)
    out = jnp.where(row == 0, hi, jnp.where(row == 1, mid, jnp.where(row == 2, lo, 0.0)))
    out = jnp.where(row == 3, member, out)
    return jnp.where((row >= 8) & (row < 11), 1.0, out)


def swapped(block):
    aug = block[DIM:AUGD].astype(F32)
    aug = jnp.concatenate([aug[8:], aug[:8]], axis=0).astype(BF16)
    return jnp.concatenate([block[:DIM], aug], axis=0)


def gauss(std, swp):
    scale = LOG2E * 4.0 / DIM
    inner = lax.dot_general(std, swp, TN, preferred_element_type=F32)
    return jnp.exp2(inner * scale)


def stack2(value):
    high, low = split2(value)
    return jnp.concatenate([high, low], axis=0)


def apply_mat(stacked, mat):
    both = jnp.dot(stacked, mat, preferred_element_type=F32)
    half = both.shape[0] // 2
    return both[:half] + both[half:]


def onehot(sel, rows):
    at = lax.broadcasted_iota(jnp.int32, (rows, sel.shape[1]), 0)
    return jnp.where(at == sel, 1.0, 0.0).astype(BF16)


def choose(points, sel):
    return jnp.dot(points, onehot(sel, points.shape[1]), preferred_element_type=F32).astype(BF16)


def body(
    y_size, z_size,
    pts_ref, chg_ref, order_ref, nbr_ref, msk_ref, lsk_ref, psk_ref, usk_ref,
    out_ref,
    win, own_swp, acc, cnt, tp, tu, n8, n4, n2, u4, u2, ups, crosses, downs, far, leaf_mats,
    wsend, wrecv, psend, precv, usend, urecv,
):
    leaf = lax.axis_index("leaf")
    sub = lax.axis_index("sub")
    leaf_count = lax.axis_size("leaf")
    device = leaf * 4 + sub
    core = leaf % 2
    z = (leaf // 2) % z_size
    y = leaf // (2 * z_size)
    prev = (leaf + leaf_count - 1) % leaf_count
    nxt = (leaf + 1) % leaf_count
    partner = leaf + 1 - 2 * core

    def x_peer(step):
        return (leaf, (sub + step) % 4)

    def z_peer(step):
        return ((y * z_size + (z + step) % z_size) * 2 + core, sub)

    def y_peer(step):
        return ((((y + step) % y_size) * z_size + z) * 2 + core, sub)

    other_core = [(partner, (sub + step) % 4) for step in (0, 1, 3, 2)]
    beyond = (leaf + leaf_count - 1 + 2 * core) % leaf_count
    stage_peers = [
        [x_peer(s) for s in (2, 1, 3)] + other_core,
        [z_peer(s) for s in (4, 3, 5, 2, 6, 1, 7)],
        [y_peer(s) for s in (4, 3, 5, 2, 6, 1, 7)],
    ]
    greet = stage_peers[2] + stage_peers[1] + stage_peers[0] + [(beyond, sub)]
    barrier = pltpu.get_barrier_semaphore()
    for peer in greet:
        pl.semaphore_signal(barrier, inc=1, device_id=peer, device_id_type=MESH)
    place8 = [core * 4 + sub, z, y]

    def tree_copies(buffer, send_sem, recv_sem, stage):
        slot = place8[stage]
        return [
            pltpu.make_async_remote_copy(
                src_ref=buffer.at[stage, slot], dst_ref=buffer.at[stage, slot],
                send_sem=send_sem.at[stage, i], recv_sem=recv_sem.at[stage, slot],
                device_id=peer, device_id_type=MESH,
            )
            for i, peer in enumerate(stage_peers[stage])
        ]

    tree_sends = []

    def tree_send(buffer, send_sem, recv_sem, stage):
        copies = tree_copies(buffer, send_sem, recv_sem, stage)
        for copy in copies:
            copy.start()
        tree_sends.extend(copies)

    def tree_wait(buffer, recv_sem, stage):
        for step in range(1, 8):
            slot = (place8[stage] + step) % 8
            pltpu.make_async_copy(
                buffer.at[stage, slot], buffer.at[stage, slot], recv_sem.at[stage, slot]
            ).wait()

    order = order_ref[...]
    pts = pts_ref[...].astype(BF16)
    own_aug = augment(pts.astype(F32), 0.0)
    own_std = jnp.concatenate([pts, own_aug.astype(BF16)], axis=0)
    coarse = (order // 32).astype(F32)
    fine = (order % 32).astype(F32)
    skels = []
    for own in range(2):
        part = slice(own * HALF, (own + 1) * HALF)
        place = jnp.concatenate([coarse[:, part], fine[:, part], jnp.zeros((6, HALF), F32)], axis=0)
        pick = onehot(lsk_ref[own : own + 1, :], HALF)
        found = jnp.dot(place.astype(BF16), pick, preferred_element_type=F32)
        where = (found[0:1] * 32.0 + found[1:2]).astype(jnp.int32)
        skels.append(choose(own_std, where))
    pair = jnp.concatenate(skels, axis=1)
    node = choose(pair, psk_ref[...])
    tp[0, pl.ds(place8[0], 1)] = node[None, 0:DIM]

    pl.semaphore_wait(barrier, len(greet))
    tree_send(tp, psend, precv, 0)

    second = order[:, HALF:]
    grid = lax.dot_general(
        onehot(second // 128, 8), onehot(second % 128, 128), NT, preferred_element_type=F32
    )
    member = jnp.concatenate([grid[k : k + 1] for k in range(8)], axis=1)
    chg_hi, chg_lo = split2(chg_ref[...])
    row = lax.broadcasted_iota(jnp.int32, (AUG, PTS), 0)
    win[4, 0:DIM] = pts
    win[4, DIM:AUGD] = jnp.where(row == 3, member, own_aug).astype(BF16)
    win[4, AUGD:WROWS] = chg_hi

    def window_copy(slot, target_slot, index, peer):
        return pltpu.make_async_remote_copy(
            src_ref=win.at[slot], dst_ref=win.at[target_slot],
            send_sem=wsend.at[index], recv_sem=wrecv.at[target_slot],
            device_id=peer, device_id_type=MESH,
        )

    sends = []
    for step in (1, 3, 2):
        sends.append(window_copy(4, 4 + (4 - step) % 4, step - 1, x_peer(step)))
    sends.append(window_copy(4, 8, 3, (prev, sub)))
    sends.append(window_copy(4, 0, 4, (nxt, sub)))
    for copy in sends:
        copy.start()

    def window_wait(slot):
        pltpu.make_async_copy(win.at[slot], win.at[slot], wrecv.at[slot]).wait()

    weights = []
    for own in range(2):
        mine = member if own else 1.0 - member
        masked = jnp.concatenate([chg_hi.astype(F32) * mine, chg_lo.astype(F32) * mine], axis=0)
        mat = gauss(own_std, swapped(skels[own])).astype(BF16)
        weights.append(stack2(apply_mat(masked.astype(BF16), mat)))
    pair_mat = gauss(pair, swapped(node)).astype(BF16)
    tu[0, pl.ds(place8[0], 1)] = stack2(
        apply_mat(jnp.concatenate(weights, axis=1), pair_mat)
    )[None]
    tree_send(tu, usend, urecv, 0)

    k = lax.broadcasted_iota(jnp.int32, (24, 32), 0)
    slot_k = k // 2
    ids = ((leaf + slot_k // 4 - 1) * 4 + (sub + slot_k % 4) % 4) * 2 + k % 2
    for own in range(2):
        hit = jnp.where(nbr_ref[own : own + 1, :] == ids, msk_ref[own : own + 1, :], 0)
        total = jnp.sum(hit.astype(F32), axis=1, keepdims=True)
        cnt[own] = jnp.broadcast_to(total, (24, 128))

    own_swp[...] = swapped(own_std)
    for own in range(2):
        leaf_mats[own, :, 0:PTS] = gauss(skels[own], own_swp[...]).astype(BF16)
        leaf_mats[own, :, PTS:] = gauss(node, swapped(skels[own])).astype(BF16)
        mat = gauss(skels[1 - own], swapped(skels[own])).astype(BF16)
        far[9 + own] = apply_mat(weights[1 - own], mat)

    acc[...] = jnp.zeros_like(acc)

    def near(slot):
        aug = win[slot, DIM:AUGD].astype(F32)
        group = aug[3:4]
        charge = win[slot, AUGD:WROWS].astype(F32)
        rows = []
        for own in range(2):
            c0 = cnt[own, pl.ds(2 * slot, 1), 0:1]
            c1 = cnt[own, pl.ds(2 * slot + 1, 1), 0:1]
            rows.append(charge * (c0 + (c1 - c0) * group))
        rows = jnp.concatenate(rows, axis=0).astype(BF16)
        mat = gauss(win[slot, 0:AUGD], own_swp[...]).astype(BF16)
        acc[...] += jnp.dot(rows, mat, preferred_element_type=F32)

    def select_stage(stage):
        firsts = [(256, 128, 64), (32, 16, 8), (4, 2, 0)][stage]
        base = [device // 8, device // 64, 0 * device][stage]
        tree_wait(tp, precv, stage)
        nodes = []
        for j in range(8):
            pts = tp[stage, j]
            nodes.append(
                jnp.concatenate([pts, augment(pts.astype(F32), 0.0).astype(BF16)], axis=0)
            )
            n8[stage, j] = nodes[-1]
        for depth, kept in ((0, n4), (1, n2), (2, None)):
            if depth == 2 and stage == 2:
                break
            count = len(nodes) // 2
            pairs = [jnp.concatenate(nodes[2 * j : 2 * j + 2], axis=1) for j in range(count)]
            nodes = []
            for j in range(count):
                sel = usk_ref[pl.ds(firsts[depth] + base * count + j, 1), :]
                nodes.append(choose(pairs[j], sel))
                if kept is not None:
                    kept[stage, j] = nodes[-1]
        if stage < 2:
            tp[stage + 1, pl.ds(place8[stage + 1], 1)] = nodes[0][None, 0:DIM]
            tree_send(tp, psend, precv, stage + 1)
            return nodes[0]
        return None

    def pair_of(buffer, stage, j):
        return jnp.concatenate([buffer[stage, 2 * j], buffer[stage, 2 * j + 1]], axis=1)

    def path_of(stage):
        a = place8[stage]
        b, c = a // 2, a // 4
        return (a, a + 1 - 2 * (a % 2)), (b, b + 1 - 2 * (b % 2)), (c, 1 - c)

    def matrices(stage, top):
        for j in range(4):
            ups[stage, j] = gauss(pair_of(n8, stage, j), swapped(n4[stage, j])).astype(BF16)
        for j in range(2):
            ups[stage, 4 + j] = gauss(pair_of(n4, stage, j), swapped(n2[stage, j])).astype(BF16)
        if top is not None:
            ups[stage, 6] = gauss(pair_of(n2, stage, 0), swapped(top)).astype(BF16)
        (a, a1), (b, b1), (c, c1) = path_of(stage)
        node8, node4, node2 = n8[stage, a], n4[stage, b], n2[stage, c]
        crosses[3 * stage] = gauss(n8[stage, a1], swapped(node8)).astype(BF16)
        crosses[3 * stage + 1] = gauss(n4[stage, b1], swapped(node4)).astype(BF16)
        crosses[3 * stage + 2] = gauss(n2[stage, c1], swapped(node2)).astype(BF16)
        downs[3 * stage] = gauss(node4, swapped(node8)).astype(BF16)
        downs[3 * stage + 1] = gauss(node2, swapped(node4)).astype(BF16)
        if top is not None:
            downs[3 * stage + 2] = gauss(top, swapped(node2)).astype(BF16)

    def weights_stage(stage):
        tree_wait(tu, urecv, stage)
        for j in range(4):
            u4[stage, j] = stack2(apply_mat(pair_of(tu, stage, j), ups[stage, j]))
        for j in range(2):
            u2[stage, j] = stack2(apply_mat(pair_of(u4, stage, j), ups[stage, 4 + j]))
        if stage < 2:
            top = stack2(apply_mat(pair_of(u2, stage, 0), ups[stage, 6]))
            tu[stage + 1, pl.ds(place8[stage + 1], 1)] = top[None]
            tree_send(tu, usend, urecv, stage + 1)
        (a, a1), (b, b1), (c, c1) = path_of(stage)
        far[3 * stage] = apply_mat(tu[stage, a1], crosses[3 * stage])
        far[3 * stage + 1] = apply_mat(u4[stage, b1], crosses[3 * stage + 1])
        far[3 * stage + 2] = apply_mat(u2[stage, c1], crosses[3 * stage + 2])

    near(4)
    top = select_stage(0)
    matrices(0, top)
    weights_stage(0)

    relays = []
    for i, dx in enumerate((1, 3, 2)):
        window_wait(4 + dx)
        relays.append(window_copy(4 + dx, 8 + dx, 5 + 2 * i, (prev, sub)))
        relays.append(window_copy(4 + dx, dx, 6 + 2 * i, (nxt, sub)))
        relays[-2].start()
        relays[-1].start()

    def group_block(i, carry):
        near(4 + i)
        return carry

    def gray(i):
        return i + (i // 2) * (1 - 2 * (i % 2))

    def partner_block(i, carry):
        slot = gray(i) + 8 * (1 - core)
        window_wait(slot)
        near(slot)
        return carry

    def beyond_block(i, carry):
        slot = gray(i) + 8 * core
        window_wait(slot)
        near(slot)
        return carry

    lax.fori_loop(1, 4, group_block, 0)
    lax.fori_loop(0, 4, partner_block, 0)
    top = select_stage(1)
    matrices(1, top)
    weights_stage(1)
    lax.fori_loop(0, 4, beyond_block, 0)
    select_stage(2)
    matrices(2, None)
    weights_stage(2)

    value = far[8]
    for index in range(7, -1, -1):
        value = far[index] + apply_mat(stack2(value), downs[index])
    for own in range(2):
        term = far[9 + own] + apply_mat(stack2(value), leaf_mats[own, :, PTS:])
        acc[own * RHS : (own + 1) * RHS] += apply_mat(stack2(term), leaf_mats[own, :, 0:PTS])

    mine = win[4, DIM:AUGD].astype(F32)[3:4]
    out_ref[...] = jnp.where(mine > 0.5, acc[RHS:], acc[:RHS])

    for copy in sends + relays + tree_sends:
        copy.wait_send()


def shards(points, charges, order, neighbours, neighbour_mask, leaf_skel, pair_skel, upper_skel):
    call = pl.pallas_call(
        functools.partial(body, 8, 8),
        out_shape=jax.ShapeDtypeStruct((RHS, PTS), F32),
        in_specs=[pl.BlockSpec(memory_space=pltpu.VMEM)] * 8,
        out_specs=pl.BlockSpec(memory_space=pltpu.VMEM),
        scratch_shapes=[
            pltpu.VMEM((12, WROWS, PTS), BF16),
            pltpu.VMEM((AUGD, PTS), BF16),
            pltpu.VMEM((2 * RHS, PTS), F32),
            pltpu.VMEM((2, 24, 128), F32),
            pltpu.VMEM((3, 8, DIM, SKEL), BF16),
            pltpu.VMEM((3, 8, UROWS, SKEL), BF16),
            pltpu.VMEM((3, 8, AUGD, SKEL), BF16),
            pltpu.VMEM((3, 4, AUGD, SKEL), BF16),
            pltpu.VMEM((3, 2, AUGD, SKEL), BF16),
            pltpu.VMEM((3, 4, UROWS, SKEL), BF16),
            pltpu.VMEM((3, 2, UROWS, SKEL), BF16),
            pltpu.VMEM((3, 7, 2 * SKEL, SKEL), BF16),
            pltpu.VMEM((9, SKEL, SKEL), BF16),
            pltpu.VMEM((8, SKEL, SKEL), BF16),
            pltpu.VMEM((11, RHS, SKEL), F32),
            pltpu.VMEM((2, SKEL, PTS + SKEL), BF16),
            pltpu.SemaphoreType.DMA((11,)),
            pltpu.SemaphoreType.DMA((12,)),
            pltpu.SemaphoreType.DMA((3, 7)),
            pltpu.SemaphoreType.DMA((3, 8)),
            pltpu.SemaphoreType.DMA((3, 7)),
            pltpu.SemaphoreType.DMA((3, 8)),
        ],
        compiler_params=pltpu.CompilerParams(
            collective_id=0, has_side_effects=True, vmem_limit_bytes=56 << 20
        ),
        name="krr_matvec",
    )
    out = call(
        points.T, charges.T, order, neighbours, neighbour_mask, leaf_skel, pair_skel, upper_skel
    )
    return out.T


def solution(mesh):
    placed = (P(("leaf", "sub"), None),) * 7 + (P(),)
    return jax.shard_map(
        shards, mesh=mesh, in_specs=placed, out_specs=P(("leaf", "sub"), None), check_vma=False
    )
```

```python
import functools

import jax
import jax.numpy as jnp
from jax import lax
from jax.experimental import pallas as pl
from jax.experimental.pallas import tpu as pltpu
from jax.sharding import PartitionSpec as P

F32 = jnp.float32
BF16 = jnp.bfloat16
MESH = pl.DeviceIdType.MESH
TN = (((0,), (0,)), ((), ()))
NT = (((1,), (1,)), ((), ()))
LOG2E = 1.4426950408889634

DIM = 64
AUG = 16
RHS = 16
PTS = 1024
SKEL = 128
HALF = PTS // 2
AUGD = DIM + AUG
WROWS = AUGD + RHS
UROWS = 2 * RHS


def split2(value):
    high = value.astype(BF16)
    return high, (value - high.astype(F32)).astype(BF16)


def split3(value):
    high = value.astype(BF16)
    rest = value - high.astype(F32)
    mid = rest.astype(BF16)
    return high.astype(F32), mid.astype(F32), (rest - mid.astype(F32)).astype(BF16).astype(F32)


def augment(pts_f32, member):
    width = pts_f32.shape[1]
    n = -0.5 * jnp.sum(pts_f32 * pts_f32, axis=0, keepdims=True)
    hi, mid, lo = split3(n)
    row = lax.broadcasted_iota(jnp.int32, (AUG, width), 0)
    out = jnp.where(row == 0, hi, jnp.where(row == 1, mid, jnp.where(row == 2, lo, 0.0)))
    out = jnp.where(row == 3, member, out)
    return jnp.where((row >= 8) & (row < 11), 1.0, out)


def swapped(block):
    aug = block[DIM:AUGD].astype(F32)
    aug = jnp.concatenate([aug[8:], aug[:8]], axis=0).astype(BF16)
    return jnp.concatenate([block[:DIM], aug], axis=0)


def gauss(std, swp):
    scale = LOG2E * 4.0 / DIM
    inner = lax.dot_general(std, swp, TN, preferred_element_type=F32)
    return jnp.exp2(inner * scale)


def stack2(value):
    high, low = split2(value)
    return jnp.concatenate([high, low], axis=0)


def apply_mat(stacked, mat):
    both = jnp.dot(stacked, mat, preferred_element_type=F32)
    half = both.shape[0] // 2
    return both[:half] + both[half:]


def onehot(sel, rows):
    at = lax.broadcasted_iota(jnp.int32, (rows, sel.shape[1]), 0)
    return jnp.where(at == sel, 1.0, 0.0).astype(BF16)


def choose(points, sel):
    return jnp.dot(points, onehot(sel, points.shape[1]), preferred_element_type=F32).astype(BF16)


def lookup(table, sel):
    pad = jnp.zeros((6, table.shape[1]), F32)
    rows = jnp.concatenate([(table >> 5).astype(F32), (table & 31).astype(F32), pad], axis=0)
    found = jnp.dot(rows.astype(BF16), onehot(sel, table.shape[1]), preferred_element_type=F32)
    return (found[0:1] * 32.0 + found[1:2]).astype(jnp.int32)


def body(
    y_size, z_size,
    pts_ref, chg_ref, order_ref, nbr_ref, msk_ref, lsk_ref, psk_ref, usk_ref,
    out_ref,
    win, own_swp, acc, cnt, tp, tu, n8, n4, n2, u4, u2, ups, crosses, downs, far, leaf_mats, tops, upper,
    wsend, wrecv, psend, precv, usend, urecv, near_in, far_in,
):
    leaf = lax.axis_index("leaf")
    sub = lax.axis_index("sub")
    leaf_count = lax.axis_size("leaf")
    device = leaf * 4 + sub
    core = leaf % 2
    z = (leaf // 2) % z_size
    y = leaf // (2 * z_size)
    partner = leaf + 1 - 2 * core

    def x_peer(step):
        return (leaf, (sub + step) % 4)

    def z_peer(step):
        return ((y * z_size + (z + step) % z_size) * 2 + core, sub)

    def y_peer(step):
        return ((((y + step) % y_size) * z_size + z) * 2 + core, sub)

    other_core = [(partner, (sub + step) % 4) for step in (0, 1, 3, 2)]
    beyond = (leaf + leaf_count - 1 + 2 * core) % leaf_count
    stage_peers = [
        [x_peer(s) for s in (2, 1, 3)] + other_core,
        [z_peer(s) for s in (4, 3, 5, 2, 6, 1, 7)],
        [y_peer(s) for s in (4, 3, 5, 2, 6, 1, 7)],
    ]
    barrier = pltpu.get_barrier_semaphore()
    own_chip = (leaf - core, leaf - core + 1)

    def signal(semaphore, peer):
        pl.semaphore_signal(semaphore, inc=1, device_id=peer, device_id_type=MESH)

    for step in (1, 2, 3):
        signal(barrier, (own_chip[0], (sub + step) % 4))

    @pl.when(core == 1)
    def _():
        signal(barrier, (own_chip[0], sub))

    for step in range(1, 8):
        signal(barrier, ((y * z_size + (z + step) % z_size) * 2 + 1, sub))
        signal(barrier, ((((y + step) % y_size) * z_size + z) * 2 + 1, sub))
    signal(barrier, (beyond - beyond % 2 + 1, sub))

    def group_entered():
        @pl.when(core == 0)
        def _():
            pl.semaphore_wait(barrier, 7)
            signal(near_in, (own_chip[1], sub))

        @pl.when(core == 1)
        def _():
            pl.semaphore_wait(near_in, 1)

    def far_entered():
        @pl.when(core == 1)
        def _():
            pl.semaphore_wait(barrier, 2 * (z_size - 1) + 2 * (y_size - 1) + 2)
            signal(far_in, (own_chip[0], sub))

        @pl.when(core == 0)
        def _():
            pl.semaphore_wait(far_in, 1)

    place8 = [core * 4 + sub, z, y]

    def tree_copies(buffer, send_sem, recv_sem, stage):
        slot = place8[stage]
        return [
            pltpu.make_async_remote_copy(
                src_ref=buffer.at[stage, slot], dst_ref=buffer.at[stage, slot],
                send_sem=send_sem.at[stage, i], recv_sem=recv_sem.at[stage, slot],
                device_id=peer, device_id_type=MESH,
            )
            for i, peer in enumerate(stage_peers[stage])
        ]

    tree_sends = []

    def tree_send(buffer, send_sem, recv_sem, stage):
        copies = tree_copies(buffer, send_sem, recv_sem, stage)
        for copy in copies:
            copy.start()
        tree_sends.extend(copies)

    def tree_wait(buffer, recv_sem, stage):
        for step in range(1, 8):
            slot = (place8[stage] + step) % 8
            pltpu.make_async_copy(
                buffer.at[stage, slot], buffer.at[stage, slot], recv_sem.at[stage, slot]
            ).wait()

    order = order_ref[...]
    pts = pts_ref[...].astype(BF16)
    own_aug = augment(pts.astype(F32), 0.0)
    own_std = jnp.concatenate([pts, own_aug.astype(BF16)], axis=0)
    skels = []
    for own in range(2):
        where = lookup(order[:, own * HALF : (own + 1) * HALF], lsk_ref[own : own + 1, :])
        skels.append(choose(own_std, where))
    pair = jnp.concatenate(skels, axis=1)
    node = choose(pair, psk_ref[...])
    tp[0, pl.ds(place8[0], 1)] = node[None, 0:DIM]

    group_entered()
    tree_send(tp, psend, precv, 0)

    second = order[:, HALF:]
    grid = lax.dot_general(
        onehot(second >> 7, 8), onehot(second & 127, 128), NT, preferred_element_type=F32
    )
    member = jnp.concatenate([grid[k : k + 1] for k in range(8)], axis=1)
    chg_hi, chg_lo = split2(chg_ref[...])
    row = lax.broadcasted_iota(jnp.int32, (AUG, PTS), 0)
    win[4, 0:DIM] = pts
    win[4, DIM:AUGD] = jnp.where(row == 3, member, own_aug).astype(BF16)
    win[4, AUGD:WROWS] = chg_hi

    def window_copy(slot, target_slot, index, peer):
        return pltpu.make_async_remote_copy(
            src_ref=win.at[slot], dst_ref=win.at[target_slot],
            send_sem=wsend.at[index], recv_sem=wrecv.at[target_slot],
            device_id=peer, device_id_type=MESH,
        )

    ours, theirs = 8 * core, 8 * (1 - core)
    sends = []

    def window_send(*args):
        sends.append(window_copy(*args))
        sends[-1].start()

    window_send(4, ours, 1, (partner, sub))

    def window_wait(slot):
        pltpu.make_async_copy(win.at[slot], win.at[slot], wrecv.at[slot]).wait()

    weights = []
    for own in range(2):
        mine = member if own else 1.0 - member
        masked = jnp.concatenate([chg_hi.astype(F32) * mine, chg_lo.astype(F32) * mine], axis=0)
        mat = gauss(own_std, swapped(skels[own])).astype(BF16)
        weights.append(stack2(apply_mat(masked.astype(BF16), mat)))
    pair_mat = gauss(pair, swapped(node)).astype(BF16)
    tu[0, pl.ds(place8[0], 1)] = stack2(
        apply_mat(jnp.concatenate(weights, axis=1), pair_mat)
    )[None]
    tree_send(tu, usend, urecv, 0)
    for step in (2, 1, 3):
        window_send(4, 4 + (4 - step) % 4, 1 + step, x_peer(step))

    k = lax.broadcasted_iota(jnp.int32, (24, 32), 0)
    slot_k = k // 2
    ids = ((leaf + slot_k // 4 - 1) * 4 + (sub + slot_k % 4) % 4) * 2 + k % 2
    for own in range(2):
        hit = jnp.where(nbr_ref[own : own + 1, :] == ids, msk_ref[own : own + 1, :], 0)
        total = jnp.sum(hit.astype(F32), axis=1, keepdims=True)
        cnt[own] = jnp.broadcast_to(total, (24, 128))

    own_swp[...] = swapped(own_std)
    for own in range(2):
        leaf_mats[own, :, 0:PTS] = gauss(skels[own], own_swp[...]).astype(BF16)
        leaf_mats[own, :, PTS:] = gauss(node, swapped(skels[own])).astype(BF16)
        mat = gauss(skels[1 - own], swapped(skels[own])).astype(BF16)
        far[9 + own] = apply_mat(weights[1 - own], mat)

    acc[...] = jnp.zeros_like(acc)

    def near(slot):
        aug = win[slot, DIM:AUGD].astype(F32)
        group = aug[3:4]
        charge = win[slot, AUGD:WROWS].astype(F32)
        rows = []
        for own in range(2):
            c0 = cnt[own, pl.ds(2 * slot, 1), 0:1]
            c1 = cnt[own, pl.ds(2 * slot + 1, 1), 0:1]
            rows.append(charge * (c0 + (c1 - c0) * group))
        rows = jnp.concatenate(rows, axis=0).astype(BF16)
        mat = gauss(win[slot, 0:AUGD], own_swp[...]).astype(BF16)
        acc[...] += jnp.dot(rows, mat, preferred_element_type=F32)

    firsts = [(256, 128, 64), (32, 16, 8), (4, 2, 0)]
    bases = [device // 8, device // 64, 0 * device]

    def chosen_rows(stage, depth):
        count = 4 >> depth
        start = firsts[stage][depth] + bases[stage] * count
        return [usk_ref[pl.ds(start + j, 1), :] for j in range(count)]

    def compose(stage):
        at = [sel + 256 * j for j, sel in enumerate(chosen_rows(stage, 0))]
        for depth in (1, 2):
            at = [
                lookup(jnp.concatenate(at[2 * j : 2 * j + 2], axis=1), sel)
                for j, sel in enumerate(chosen_rows(stage, depth))
            ]
        tops[stage] = onehot(at[0], 8 * SKEL)

    def select_stage(stage):
        tree_wait(tp, precv, stage)
        raw = [tp[stage, j] for j in range(8)]
        if stage < 2:
            wide = jnp.concatenate(raw, axis=1)
            top = jnp.dot(wide, tops[stage], preferred_element_type=F32).astype(BF16)
            tp[stage + 1, pl.ds(place8[stage + 1], 1)] = top[None]
            if stage == 0:
                far_entered()
            tree_send(tp, psend, precv, stage + 1)
            if stage == 0:
                window_send(4, theirs, 0, (beyond, sub))
        nodes = []
        for j in range(8):
            rows = augment(raw[j].astype(F32), 0.0).astype(BF16)
            nodes.append(jnp.concatenate([raw[j], rows], axis=0))
            n8[stage, j] = nodes[-1]
        for depth, kept in ((0, n4), (1, n2)):
            sels = chosen_rows(stage, depth)
            nodes = [
                choose(jnp.concatenate(nodes[2 * j : 2 * j + 2], axis=1), sel)
                for j, sel in enumerate(sels)
            ]
            for j, found in enumerate(nodes):
                kept[stage, j] = found
        if stage < 2:
            return choose(jnp.concatenate(nodes, axis=1), chosen_rows(stage, 2)[0])
        return None

    def pair_of(buffer, stage, j):
        return jnp.concatenate([buffer[stage, 2 * j], buffer[stage, 2 * j + 1]], axis=1)

    def path_of(stage):
        a = place8[stage]
        b, c = a // 2, a // 4
        return (a, a + 1 - 2 * (a % 2)), (b, b + 1 - 2 * (b % 2)), (c, 1 - c)

    def matrices(stage, top):
        for j in range(4):
            ups[stage, j] = gauss(pair_of(n8, stage, j), swapped(n4[stage, j])).astype(BF16)
        for j in range(2):
            ups[stage, 4 + j] = gauss(pair_of(n4, stage, j), swapped(n2[stage, j])).astype(BF16)
        if top is not None:
            ups[stage, 6] = gauss(pair_of(n2, stage, 0), swapped(top)).astype(BF16)
        (a, a1), (b, b1), (c, c1) = path_of(stage)
        node8, node4, node2 = n8[stage, a], n4[stage, b], n2[stage, c]
        crosses[3 * stage] = gauss(n8[stage, a1], swapped(node8)).astype(BF16)
        crosses[3 * stage + 1] = gauss(n4[stage, b1], swapped(node4)).astype(BF16)
        crosses[3 * stage + 2] = gauss(n2[stage, c1], swapped(node2)).astype(BF16)
        downs[3 * stage] = gauss(node4, swapped(node8)).astype(BF16)
        downs[3 * stage + 1] = gauss(node2, swapped(node4)).astype(BF16)
        if top is not None:
            downs[3 * stage + 2] = gauss(top, swapped(node2)).astype(BF16)

    def weights_stage(stage):
        tree_wait(tu, urecv, stage)
        for j in range(4):
            u4[stage, j] = stack2(apply_mat(pair_of(tu, stage, j), ups[stage, j]))
        for j in range(2):
            u2[stage, j] = stack2(apply_mat(pair_of(u4, stage, j), ups[stage, 4 + j]))
        if stage < 2:
            top = stack2(apply_mat(pair_of(u2, stage, 0), ups[stage, 6]))
            tu[stage + 1, pl.ds(place8[stage + 1], 1)] = top[None]
            tree_send(tu, usend, urecv, stage + 1)
        (a, a1), (b, b1), (c, c1) = path_of(stage)
        far[3 * stage] = apply_mat(tu[stage, a1], crosses[3 * stage])
        far[3 * stage + 1] = apply_mat(u4[stage, b1], crosses[3 * stage + 1])
        far[3 * stage + 2] = apply_mat(u2[stage, c1], crosses[3 * stage + 2])

    def way_down():
        value = far[5]
        for index in range(4, -1, -1):
            value = far[index] + apply_mat(stack2(value), downs[index])
        mat = downs[5].astype(F32)
        for index in range(4, -1, -1):
            mat = apply_mat(stack2(mat), downs[index])
        mat = stack2(mat)
        for own in range(2):
            to_leaf, to_points = leaf_mats[own, :, PTS:], leaf_mats[own, :, 0:PTS]
            term = far[9 + own] + apply_mat(stack2(value), to_leaf)
            acc[own * RHS : (own + 1) * RHS] += apply_mat(stack2(term), to_points)
            upper[own] = apply_mat(stack2(apply_mat(mat, to_leaf)), to_points).astype(BF16)

    compose(0)
    compose(1)
    near(4)
    top = select_stage(0)
    matrices(0, top)
    weights_stage(0)

    def group_block(i, carry):
        near(4 + i)
        return carry

    def gray(i):
        return i + (i // 2) * (1 - 2 * (i % 2))

    def partner_block(i, carry):
        slot = gray(i) + theirs
        window_wait(slot)
        near(slot)
        return carry

    def beyond_block(i, carry):
        slot = gray(i) + ours
        window_wait(slot)
        near(slot)
        return carry

    window_wait(theirs)
    near(theirs)
    window_wait(ours)
    near(ours)
    for dx in (1, 3, 2):
        window_wait(4 + dx)
        window_send(4 + dx, theirs + dx, 4 + dx, (beyond, sub))
        window_send(4 + dx, ours + dx, 7 + dx, (partner, sub))
    lax.fori_loop(1, 4, group_block, 0)
    top = select_stage(1)
    matrices(1, top)
    weights_stage(1)
    lax.fori_loop(1, 4, partner_block, 0)
    way_down()
    select_stage(2)
    matrices(2, None)
    weights_stage(2)
    lax.fori_loop(1, 4, beyond_block, 0)

    value = far[8]
    for index in (7, 6):
        value = far[index] + apply_mat(stack2(value), downs[index])
    stacked = stack2(value)
    for own in range(2):
        acc[own * RHS : (own + 1) * RHS] += apply_mat(stacked, upper[own])

    mine = win[4, DIM:AUGD].astype(F32)[3:4]
    out_ref[...] = jnp.where(mine > 0.5, acc[RHS:], acc[:RHS])

    for copy in sends + tree_sends:
        copy.wait_send()


def shards(points, charges, order, neighbours, neighbour_mask, leaf_skel, pair_skel, upper_skel):
    call = pl.pallas_call(
        functools.partial(body, 8, 8),
        out_shape=jax.ShapeDtypeStruct((RHS, PTS), F32),
        in_specs=[pl.BlockSpec(memory_space=pltpu.VMEM)] * 8,
        out_specs=pl.BlockSpec(memory_space=pltpu.VMEM),
        scratch_shapes=[
            pltpu.VMEM((12, WROWS, PTS), BF16),
            pltpu.VMEM((AUGD, PTS), BF16),
            pltpu.VMEM((2 * RHS, PTS), F32),
            pltpu.VMEM((2, 24, 128), F32),
            pltpu.VMEM((3, 8, DIM, SKEL), BF16),
            pltpu.VMEM((3, 8, UROWS, SKEL), BF16),
            pltpu.VMEM((3, 8, AUGD, SKEL), BF16),
            pltpu.VMEM((3, 4, AUGD, SKEL), BF16),
            pltpu.VMEM((3, 2, AUGD, SKEL), BF16),
            pltpu.VMEM((3, 4, UROWS, SKEL), BF16),
            pltpu.VMEM((3, 2, UROWS, SKEL), BF16),
            pltpu.VMEM((3, 7, 2 * SKEL, SKEL), BF16),
            pltpu.VMEM((9, SKEL, SKEL), BF16),
            pltpu.VMEM((8, SKEL, SKEL), BF16),
            pltpu.VMEM((11, RHS, SKEL), F32),
            pltpu.VMEM((2, SKEL, PTS + SKEL), BF16),
            pltpu.VMEM((2, 8 * SKEL, SKEL), BF16),
            pltpu.VMEM((2, SKEL, PTS), BF16),
            pltpu.SemaphoreType.DMA((11,)),
            pltpu.SemaphoreType.DMA((12,)),
            pltpu.SemaphoreType.DMA((3, 7)),
            pltpu.SemaphoreType.DMA((3, 8)),
            pltpu.SemaphoreType.DMA((3, 7)),
            pltpu.SemaphoreType.DMA((3, 8)),
            pltpu.SemaphoreType.REGULAR,
            pltpu.SemaphoreType.REGULAR,
        ],
        compiler_params=pltpu.CompilerParams(
            collective_id=0, has_side_effects=True, vmem_limit_bytes=56 << 20
        ),
        name="krr_matvec",
    )
    out = call(
        points.T, charges.T, order, neighbours, neighbour_mask, leaf_skel, pair_skel, upper_skel
    )
    return out.T


def solution(mesh):
    placed = (P(("leaf", "sub"), None),) * 7 + (P(),)
    return jax.shard_map(
        shards, mesh=mesh, in_specs=placed, out_specs=P(("leaf", "sub"), None), check_vma=False
    )
```

```python
import functools

import jax
import jax.numpy as jnp
from jax import lax
from jax.experimental import pallas as pl
from jax.experimental.pallas import tpu as pltpu
from jax.sharding import PartitionSpec as P

F32 = jnp.float32
BF16 = jnp.bfloat16
MESH = pl.DeviceIdType.MESH
TN = (((0,), (0,)), ((), ()))
NT = (((1,), (1,)), ((), ()))
LOG2E = 1.4426950408889634

DIM = 64
AUG = 16
RHS = 16
PTS = 1024
SKEL = 128
HALF = PTS // 2
AUGD = DIM + AUG
WROWS = AUGD + RHS
UROWS = 2 * RHS


def split2(value):
    high = value.astype(BF16)
    return high, (value - high.astype(F32)).astype(BF16)


def split3(value):
    high = value.astype(BF16)
    rest = value - high.astype(F32)
    mid = rest.astype(BF16)
    return high.astype(F32), mid.astype(F32), (rest - mid.astype(F32)).astype(BF16).astype(F32)


def augment(pts_f32, member):
    width = pts_f32.shape[1]
    n = -0.5 * jnp.sum(pts_f32 * pts_f32, axis=0, keepdims=True)
    hi, mid, lo = split3(n)
    row = lax.broadcasted_iota(jnp.int32, (AUG, width), 0)
    out = jnp.where(row == 0, hi, jnp.where(row == 1, mid, jnp.where(row == 2, lo, 0.0)))
    out = jnp.where(row == 3, member, out)
    return jnp.where((row >= 8) & (row < 11), 1.0, out)


def swapped(block):
    aug = block[DIM:AUGD].astype(F32)
    aug = jnp.concatenate([aug[8:], aug[:8]], axis=0).astype(BF16)
    return jnp.concatenate([block[:DIM], aug], axis=0)


def gauss(std, swp):
    scale = LOG2E * 4.0 / DIM
    inner = lax.dot_general(std, swp, TN, preferred_element_type=F32)
    return jnp.exp2(inner * scale)


def stack2(value):
    high, low = split2(value)
    return jnp.concatenate([high, low], axis=0)


def apply_mat(stacked, mat):
    both = jnp.dot(stacked, mat, preferred_element_type=F32)
    half = both.shape[0] // 2
    return both[:half] + both[half:]


def onehot(sel, rows):
    at = lax.broadcasted_iota(jnp.int32, (rows, sel.shape[1]), 0)
    return jnp.where(at == sel, 1.0, 0.0).astype(BF16)


def choose(points, sel):
    return jnp.dot(points, onehot(sel, points.shape[1]), preferred_element_type=F32).astype(BF16)


def lookup(table, sel):
    pad = jnp.zeros((6, table.shape[1]), F32)
    rows = jnp.concatenate([(table >> 5).astype(F32), (table & 31).astype(F32), pad], axis=0)
    found = jnp.dot(rows.astype(BF16), onehot(sel, table.shape[1]), preferred_element_type=F32)
    return (found[0:1] * 32.0 + found[1:2]).astype(jnp.int32)


def body(
    y_size, z_size,
    pts_ref, chg_ref, order_ref, nbr_ref, msk_ref, lsk_ref, psk_ref, usk_ref,
    out_ref,
    win, own_swp, acc, cnt, tp, tu, n8, n4, n2, u4, u2, ups, crosses, downs, far, leaf_mats, tops, upper,
    wsend, wrecv, psend, precv, usend, urecv, near_in, far_in,
):
    leaf = lax.axis_index("leaf")
    sub = lax.axis_index("sub")
    leaf_count = lax.axis_size("leaf")
    device = leaf * 4 + sub
    core = leaf % 2
    z = (leaf // 2) % z_size
    y = leaf // (2 * z_size)
    partner = leaf + 1 - 2 * core

    def x_peer(step):
        return (leaf, (sub + step) % 4)

    def z_peer(step):
        return ((y * z_size + (z + step) % z_size) * 2 + core, sub)

    def y_peer(step):
        return ((((y + step) % y_size) * z_size + z) * 2 + core, sub)

    other_core = [(partner, (sub + step) % 4) for step in (0, 1, 3, 2)]
    beyond = (leaf + leaf_count - 1 + 2 * core) % leaf_count
    stage_peers = [
        [x_peer(s) for s in (2, 1, 3)] + other_core,
        [z_peer(s) for s in (4, 3, 5, 2, 6, 1, 7)],
        [y_peer(s) for s in (4, 3, 5, 2, 6, 1, 7)],
    ]
    barrier = pltpu.get_barrier_semaphore()
    own_chip = (leaf - core, leaf - core + 1)

    def signal(semaphore, peer):
        pl.semaphore_signal(semaphore, inc=1, device_id=peer, device_id_type=MESH)

    for step in (1, 2, 3):
        signal(barrier, (own_chip[0], (sub + step) % 4))

    @pl.when(core == 1)
    def _():
        signal(barrier, (own_chip[0], sub))

    for step in range(1, 8):
        signal(barrier, ((y * z_size + (z + step) % z_size) * 2 + 1, sub))
        signal(barrier, ((((y + step) % y_size) * z_size + z) * 2 + 1, sub))
    signal(barrier, (beyond - beyond % 2 + 1, sub))

    def group_entered():
        @pl.when(core == 0)
        def _():
            pl.semaphore_wait(barrier, 7)
            signal(near_in, (own_chip[1], sub))

        @pl.when(core == 1)
        def _():
            pl.semaphore_wait(near_in, 1)

    def far_entered():
        @pl.when(core == 1)
        def _():
            pl.semaphore_wait(barrier, 2 * (z_size - 1) + 2 * (y_size - 1) + 2)
            signal(far_in, (own_chip[0], sub))

        @pl.when(core == 0)
        def _():
            pl.semaphore_wait(far_in, 1)

    place8 = [core * 4 + sub, z, y]

    def tree_copies(buffer, send_sem, recv_sem, stage):
        slot = place8[stage]
        return [
            pltpu.make_async_remote_copy(
                src_ref=buffer.at[stage, slot], dst_ref=buffer.at[stage, slot],
                send_sem=send_sem.at[stage, i], recv_sem=recv_sem.at[stage, slot],
                device_id=peer, device_id_type=MESH,
            )
            for i, peer in enumerate(stage_peers[stage])
        ]

    tree_sends = []

    def tree_send(buffer, send_sem, recv_sem, stage):
        copies = tree_copies(buffer, send_sem, recv_sem, stage)
        for copy in copies:
            copy.start()
        tree_sends.extend(copies)

    def tree_wait(buffer, recv_sem, stage):
        for step in range(1, 8):
            slot = (place8[stage] + step) % 8
            pltpu.make_async_copy(
                buffer.at[stage, slot], buffer.at[stage, slot], recv_sem.at[stage, slot]
            ).wait()

    order = order_ref[...]
    pts = pts_ref[...].astype(BF16)
    own_aug = augment(pts.astype(F32), 0.0)
    own_std = jnp.concatenate([pts, own_aug.astype(BF16)], axis=0)
    skels = []
    for own in range(2):
        where = lookup(order[:, own * HALF : (own + 1) * HALF], lsk_ref[own : own + 1, :])
        skels.append(choose(own_std, where))
    pair = jnp.concatenate(skels, axis=1)
    node = choose(pair, psk_ref[...])
    tp[0, pl.ds(place8[0], 1)] = node[None, 0:DIM]

    group_entered()
    tree_send(tp, psend, precv, 0)

    second = order[:, HALF:]
    grid = lax.dot_general(
        onehot(second >> 7, 8), onehot(second & 127, 128), NT, preferred_element_type=F32
    )
    member = jnp.concatenate([grid[k : k + 1] for k in range(8)], axis=1)
    chg_hi, chg_lo = split2(chg_ref[...])
    row = lax.broadcasted_iota(jnp.int32, (AUG, PTS), 0)
    win[4, 0:DIM] = pts
    win[4, DIM:AUGD] = jnp.where(row == 3, member, own_aug).astype(BF16)
    win[4, AUGD:WROWS] = chg_hi

    def window_copy(slot, target_slot, index, peer):
        return pltpu.make_async_remote_copy(
            src_ref=win.at[slot], dst_ref=win.at[target_slot],
            send_sem=wsend.at[index], recv_sem=wrecv.at[target_slot],
            device_id=peer, device_id_type=MESH,
        )

    ours, theirs = 8 * core, 8 * (1 - core)
    sends = []

    def window_send(*args):
        sends.append(window_copy(*args))
        sends[-1].start()

    window_send(4, ours, 1, (partner, sub))
    for step in (1, 3):
        window_send(4, 8 - step, 1 + step, x_peer(step))

    def window_wait(slot):
        pltpu.make_async_copy(win.at[slot], win.at[slot], wrecv.at[slot]).wait()

    weights = []
    for own in range(2):
        mine = member if own else 1.0 - member
        masked = jnp.concatenate([chg_hi.astype(F32) * mine, chg_lo.astype(F32) * mine], axis=0)
        mat = gauss(own_std, swapped(skels[own])).astype(BF16)
        weights.append(stack2(apply_mat(masked.astype(BF16), mat)))
    pair_mat = gauss(pair, swapped(node)).astype(BF16)
    tu[0, pl.ds(place8[0], 1)] = stack2(
        apply_mat(jnp.concatenate(weights, axis=1), pair_mat)
    )[None]
    tree_send(tu, usend, urecv, 0)
    far_entered()
    window_send(4, theirs, 0, (beyond, sub))

    k = lax.broadcasted_iota(jnp.int32, (24, 32), 0)
    slot_k = k // 2
    ids = ((leaf + slot_k // 4 - 1) * 4 + (sub + slot_k % 4) % 4) * 2 + k % 2
    for own in range(2):
        hit = jnp.where(nbr_ref[own : own + 1, :] == ids, msk_ref[own : own + 1, :], 0)
        total = jnp.sum(hit.astype(F32), axis=1, keepdims=True)
        cnt[own] = jnp.broadcast_to(total, (24, 128))

    own_swp[...] = swapped(own_std)
    for own in range(2):
        leaf_mats[own, :, 0:PTS] = gauss(skels[own], own_swp[...]).astype(BF16)
        leaf_mats[own, :, PTS:] = gauss(node, swapped(skels[own])).astype(BF16)
        mat = gauss(skels[1 - own], swapped(skels[own])).astype(BF16)
        far[9 + own] = apply_mat(weights[1 - own], mat)

    acc[...] = jnp.zeros_like(acc)

    def near(slot):
        aug = win[slot, DIM:AUGD].astype(F32)
        group = aug[3:4]
        charge = win[slot, AUGD:WROWS].astype(F32)
        rows = []
        for own in range(2):
            c0 = cnt[own, pl.ds(2 * slot, 1), 0:1]
            c1 = cnt[own, pl.ds(2 * slot + 1, 1), 0:1]
            rows.append(charge * (c0 + (c1 - c0) * group))
        rows = jnp.concatenate(rows, axis=0).astype(BF16)
        mat = gauss(win[slot, 0:AUGD], own_swp[...]).astype(BF16)
        acc[...] += jnp.dot(rows, mat, preferred_element_type=F32)

    firsts = [(256, 128, 64), (32, 16, 8), (4, 2, 0)]
    bases = [device // 8, device // 64, 0 * device]

    def chosen_rows(stage, depth):
        count = 4 >> depth
        start = firsts[stage][depth] + bases[stage] * count
        return [usk_ref[pl.ds(start + j, 1), :] for j in range(count)]

    def compose(stage):
        at = [sel + 256 * j for j, sel in enumerate(chosen_rows(stage, 0))]
        for depth in (1, 2):
            at = [
                lookup(jnp.concatenate(at[2 * j : 2 * j + 2], axis=1), sel)
                for j, sel in enumerate(chosen_rows(stage, depth))
            ]
        tops[stage] = onehot(at[0], 8 * SKEL)

    def select_stage(stage):
        tree_wait(tp, precv, stage)
        raw = [tp[stage, j] for j in range(8)]
        if stage < 2:
            wide = jnp.concatenate(raw, axis=1)
            top = jnp.dot(wide, tops[stage], preferred_element_type=F32).astype(BF16)
            tp[stage + 1, pl.ds(place8[stage + 1], 1)] = top[None]
            tree_send(tp, psend, precv, stage + 1)
            if stage == 0:
                window_send(4, 6, 3, x_peer(2))
        nodes = []
        for j in range(8):
            rows = augment(raw[j].astype(F32), 0.0).astype(BF16)
            nodes.append(jnp.concatenate([raw[j], rows], axis=0))
            n8[stage, j] = nodes[-1]
        for depth, kept in ((0, n4), (1, n2)):
            sels = chosen_rows(stage, depth)
            nodes = [
                choose(jnp.concatenate(nodes[2 * j : 2 * j + 2], axis=1), sel)
                for j, sel in enumerate(sels)
            ]
            for j, found in enumerate(nodes):
                kept[stage, j] = found
        if stage < 2:
            return choose(jnp.concatenate(nodes, axis=1), chosen_rows(stage, 2)[0])
        return None

    def pair_of(buffer, stage, j):
        return jnp.concatenate([buffer[stage, 2 * j], buffer[stage, 2 * j + 1]], axis=1)

    def path_of(stage):
        a = place8[stage]
        b, c = a // 2, a // 4
        return (a, a + 1 - 2 * (a % 2)), (b, b + 1 - 2 * (b % 2)), (c, 1 - c)

    def matrices(stage, top):
        for j in range(4):
            ups[stage, j] = gauss(pair_of(n8, stage, j), swapped(n4[stage, j])).astype(BF16)
        for j in range(2):
            ups[stage, 4 + j] = gauss(pair_of(n4, stage, j), swapped(n2[stage, j])).astype(BF16)
        if top is not None:
            ups[stage, 6] = gauss(pair_of(n2, stage, 0), swapped(top)).astype(BF16)
        (a, a1), (b, b1), (c, c1) = path_of(stage)
        node8, node4, node2 = n8[stage, a], n4[stage, b], n2[stage, c]
        crosses[3 * stage] = gauss(n8[stage, a1], swapped(node8)).astype(BF16)
        crosses[3 * stage + 1] = gauss(n4[stage, b1], swapped(node4)).astype(BF16)
        crosses[3 * stage + 2] = gauss(n2[stage, c1], swapped(node2)).astype(BF16)
        downs[3 * stage] = gauss(node4, swapped(node8)).astype(BF16)
        downs[3 * stage + 1] = gauss(node2, swapped(node4)).astype(BF16)
        if top is not None:
            downs[3 * stage + 2] = gauss(top, swapped(node2)).astype(BF16)

    def weights_stage(stage):
        tree_wait(tu, urecv, stage)
        for j in range(4):
            u4[stage, j] = stack2(apply_mat(pair_of(tu, stage, j), ups[stage, j]))
        for j in range(2):
            u2[stage, j] = stack2(apply_mat(pair_of(u4, stage, j), ups[stage, 4 + j]))
        if stage < 2:
            top = stack2(apply_mat(pair_of(u2, stage, 0), ups[stage, 6]))
            tu[stage + 1, pl.ds(place8[stage + 1], 1)] = top[None]
            tree_send(tu, usend, urecv, stage + 1)
        (a, a1), (b, b1), (c, c1) = path_of(stage)
        far[3 * stage] = apply_mat(tu[stage, a1], crosses[3 * stage])
        far[3 * stage + 1] = apply_mat(u4[stage, b1], crosses[3 * stage + 1])
        far[3 * stage + 2] = apply_mat(u2[stage, c1], crosses[3 * stage + 2])

    def way_down():
        value = far[5]
        for index in range(4, -1, -1):
            value = far[index] + apply_mat(stack2(value), downs[index])
        mat = downs[5].astype(F32)
        for index in range(4, -1, -1):
            mat = apply_mat(stack2(mat), downs[index])
        mat = stack2(mat)
        for own in range(2):
            to_leaf, to_points = leaf_mats[own, :, PTS:], leaf_mats[own, :, 0:PTS]
            term = far[9 + own] + apply_mat(stack2(value), to_leaf)
            acc[own * RHS : (own + 1) * RHS] += apply_mat(stack2(term), to_points)
            upper[own] = apply_mat(stack2(apply_mat(mat, to_leaf)), to_points).astype(BF16)

    compose(0)
    compose(1)
    near(4)
    top = select_stage(0)
    window_wait(theirs)
    matrices(0, top)
    near(theirs)
    weights_stage(0)

    def group_block(i, carry):
        near(5 + 2 * i)
        return carry

    def partner_block(i, carry):
        slot = theirs + 1 + 2 * i
        window_wait(slot)
        near(slot)
        return carry

    def beyond_block(i, carry):
        slot = ours + 1 + 2 * i
        window_wait(slot)
        near(slot)
        return carry

    for dx in (1, 3):
        window_wait(4 + dx)
        window_send(4 + dx, ours + dx, 7 + dx, (partner, sub))
    lax.fori_loop(0, 2, group_block, 0)
    window_wait(ours)
    for step in (1, 3):
        window_send(ours, ours + (4 - step), 4 + step // 2, x_peer(step))
    near(ours)
    top = select_stage(1)
    window_wait(6)
    window_send(6, theirs + 2, 6, (beyond, sub))
    window_send(6, ours + 2, 9, (partner, sub))
    matrices(1, top)
    near(6)
    weights_stage(1)
    lax.fori_loop(0, 2, partner_block, 0)
    window_wait(theirs + 2)
    near(theirs + 2)
    way_down()
    lax.fori_loop(0, 2, beyond_block, 0)
    select_stage(2)
    window_wait(ours + 2)
    matrices(2, None)
    near(ours + 2)
    weights_stage(2)

    value = far[8]
    for index in (7, 6):
        value = far[index] + apply_mat(stack2(value), downs[index])
    stacked = stack2(value)
    for own in range(2):
        acc[own * RHS : (own + 1) * RHS] += apply_mat(stacked, upper[own])

    mine = win[4, DIM:AUGD].astype(F32)[3:4]
    out_ref[...] = jnp.where(mine > 0.5, acc[RHS:], acc[:RHS])

    for copy in sends + tree_sends:
        copy.wait_send()


def shards(points, charges, order, neighbours, neighbour_mask, leaf_skel, pair_skel, upper_skel):
    call = pl.pallas_call(
        functools.partial(body, 8, 8),
        out_shape=jax.ShapeDtypeStruct((RHS, PTS), F32),
        in_specs=[pl.BlockSpec(memory_space=pltpu.VMEM)] * 8,
        out_specs=pl.BlockSpec(memory_space=pltpu.VMEM),
        scratch_shapes=[
            pltpu.VMEM((12, WROWS, PTS), BF16),
            pltpu.VMEM((AUGD, PTS), BF16),
            pltpu.VMEM((2 * RHS, PTS), F32),
            pltpu.VMEM((2, 24, 128), F32),
            pltpu.VMEM((3, 8, DIM, SKEL), BF16),
            pltpu.VMEM((3, 8, UROWS, SKEL), BF16),
            pltpu.VMEM((3, 8, AUGD, SKEL), BF16),
            pltpu.VMEM((3, 4, AUGD, SKEL), BF16),
            pltpu.VMEM((3, 2, AUGD, SKEL), BF16),
            pltpu.VMEM((3, 4, UROWS, SKEL), BF16),
            pltpu.VMEM((3, 2, UROWS, SKEL), BF16),
            pltpu.VMEM((3, 7, 2 * SKEL, SKEL), BF16),
            pltpu.VMEM((9, SKEL, SKEL), BF16),
            pltpu.VMEM((8, SKEL, SKEL), BF16),
            pltpu.VMEM((11, RHS, SKEL), F32),
            pltpu.VMEM((2, SKEL, PTS + SKEL), BF16),
            pltpu.VMEM((2, 8 * SKEL, SKEL), BF16),
            pltpu.VMEM((2, SKEL, PTS), BF16),
            pltpu.SemaphoreType.DMA((11,)),
            pltpu.SemaphoreType.DMA((12,)),
            pltpu.SemaphoreType.DMA((3, 7)),
            pltpu.SemaphoreType.DMA((3, 8)),
            pltpu.SemaphoreType.DMA((3, 7)),
            pltpu.SemaphoreType.DMA((3, 8)),
            pltpu.SemaphoreType.REGULAR,
            pltpu.SemaphoreType.REGULAR,
        ],
        compiler_params=pltpu.CompilerParams(
            collective_id=0, has_side_effects=True, vmem_limit_bytes=56 << 20
        ),
        name="krr_matvec",
    )
    out = call(
        points.T, charges.T, order, neighbours, neighbour_mask, leaf_skel, pair_skel, upper_skel
    )
    return out.T


def solution(mesh):
    placed = (P(("leaf", "sub"), None),) * 7 + (P(),)
    return jax.shard_map(
        shards, mesh=mesh, in_specs=placed, out_specs=P(("leaf", "sub"), None), check_vma=False
    )
```

```python
import functools

import jax
import jax.numpy as jnp
from jax import lax
from jax.experimental import pallas as pl
from jax.experimental.pallas import tpu as pltpu
from jax.sharding import PartitionSpec as P

F32 = jnp.float32
BF16 = jnp.bfloat16
MESH = pl.DeviceIdType.MESH
TN = (((0,), (0,)), ((), ()))
NT = (((1,), (1,)), ((), ()))
LOG2E = 1.4426950408889634

DIM = 64
AUG = 16
RHS = 16
PTS = 1024
SKEL = 128
HALF = PTS // 2
AUGD = DIM + AUG
WROWS = AUGD + RHS
UROWS = 2 * RHS


def split2(value):
    high = value.astype(BF16)
    return high, (value - high.astype(F32)).astype(BF16)


def split3(value):
    high = value.astype(BF16)
    rest = value - high.astype(F32)
    mid = rest.astype(BF16)
    return high.astype(F32), mid.astype(F32), (rest - mid.astype(F32)).astype(BF16).astype(F32)


def augment(pts_f32, member):
    width = pts_f32.shape[1]
    n = -0.5 * jnp.sum(pts_f32 * pts_f32, axis=0, keepdims=True)
    hi, mid, lo = split3(n)
    row = lax.broadcasted_iota(jnp.int32, (AUG, width), 0)
    out = jnp.where(row == 0, hi, jnp.where(row == 1, mid, jnp.where(row == 2, lo, 0.0)))
    out = jnp.where(row == 3, member, out)
    return jnp.where((row >= 8) & (row < 11), 1.0, out)


def swapped(block):
    aug = block[DIM:AUGD].astype(F32)
    aug = jnp.concatenate([aug[8:], aug[:8]], axis=0).astype(BF16)
    return jnp.concatenate([block[:DIM], aug], axis=0)


def gauss(std, swp):
    scale = LOG2E * 4.0 / DIM
    inner = lax.dot_general(std, swp, TN, preferred_element_type=F32)
    return jnp.exp2(inner * scale)


def stack2(value):
    high, low = split2(value)
    return jnp.concatenate([high, low], axis=0)


def apply_mat(stacked, mat):
    both = jnp.dot(stacked, mat, preferred_element_type=F32)
    half = both.shape[0] // 2
    return both[:half] + both[half:]


def onehot(sel, rows):
    at = lax.broadcasted_iota(jnp.int32, (rows, sel.shape[1]), 0)
    return jnp.where(at == sel, 1.0, 0.0).astype(BF16)


def choose(points, sel):
    return jnp.dot(points, onehot(sel, points.shape[1]), preferred_element_type=F32).astype(BF16)


def lookup(table, sel):
    pad = jnp.zeros((6, table.shape[1]), F32)
    rows = jnp.concatenate([(table >> 5).astype(F32), (table & 31).astype(F32), pad], axis=0)
    found = jnp.dot(rows.astype(BF16), onehot(sel, table.shape[1]), preferred_element_type=F32)
    return (found[0:1] * 32.0 + found[1:2]).astype(jnp.int32)


def body(
    y_size, z_size,
    pts_in, chg_in, order_in, nbr_in, msk_in, lsk_in, psk_in, usk_in,
    out_ref,
    pts_ref, chg_ref, order_ref, nbr_ref, msk_ref, lsk_ref, psk_ref, usk_ref, fetched,
    win, own_swp, acc, cnt, tp, tu, n8, n4, n2, u4, u2, ups, crosses, downs, far, leaf_mats, tops, upper,
    wsend, wrecv, psend, precv, usend, urecv, near_in, far_in,
):
    leaf = lax.axis_index("leaf")
    sub = lax.axis_index("sub")
    leaf_count = lax.axis_size("leaf")
    device = leaf * 4 + sub
    core = leaf % 2
    z = (leaf // 2) % z_size
    y = leaf // (2 * z_size)
    partner = leaf + 1 - 2 * core

    def x_peer(step):
        return (leaf, (sub + step) % 4)

    def z_peer(step):
        return ((y * z_size + (z + step) % z_size) * 2 + core, sub)

    def y_peer(step):
        return ((((y + step) % y_size) * z_size + z) * 2 + core, sub)

    other_core = [(partner, (sub + step) % 4) for step in (0, 1, 3, 2)]
    beyond = (leaf + leaf_count - 1 + 2 * core) % leaf_count
    stage_peers = [
        [x_peer(s) for s in (2, 1, 3)] + other_core,
        [z_peer(s) for s in (4, 3, 5, 2, 6, 1, 7)],
        [y_peer(s) for s in (4, 3, 5, 2, 6, 1, 7)],
    ]
    barrier = pltpu.get_barrier_semaphore()
    own_chip = (leaf - core, leaf - core + 1)

    def signal(semaphore, peer):
        pl.semaphore_signal(semaphore, inc=1, device_id=peer, device_id_type=MESH)

    for step in (1, 2, 3):
        signal(barrier, (own_chip[0], (sub + step) % 4))

    @pl.when(core == 1)
    def _():
        signal(barrier, (own_chip[0], sub))

    for step in range(1, 8):
        signal(barrier, ((y * z_size + (z + step) % z_size) * 2 + 1, sub))
        signal(barrier, ((((y + step) % y_size) * z_size + z) * 2 + 1, sub))
    signal(barrier, (beyond - beyond % 2 + 1, sub))

    fetches = [
        pltpu.make_async_copy(source, target, fetched.at[i])
        for i, (source, target) in enumerate(
            (
                (order_in, order_ref), (lsk_in, lsk_ref), (psk_in, psk_ref), (pts_in, pts_ref),
                (chg_in, chg_ref), (nbr_in, nbr_ref), (msk_in, msk_ref), (usk_in, usk_ref),
            )
        )
    ]
    for copy in fetches:
        copy.start()

    def group_entered():
        @pl.when(core == 0)
        def _():
            pl.semaphore_wait(barrier, 7)
            signal(near_in, (own_chip[1], sub))

        @pl.when(core == 1)
        def _():
            pl.semaphore_wait(near_in, 1)

    def far_entered():
        @pl.when(core == 1)
        def _():
            pl.semaphore_wait(barrier, 2 * (z_size - 1) + 2 * (y_size - 1) + 2)
            signal(far_in, (own_chip[0], sub))

        @pl.when(core == 0)
        def _():
            pl.semaphore_wait(far_in, 1)

    place8 = [core * 4 + sub, z, y]

    def tree_copies(buffer, send_sem, recv_sem, stage):
        slot = place8[stage]
        return [
            pltpu.make_async_remote_copy(
                src_ref=buffer.at[stage, slot], dst_ref=buffer.at[stage, slot],
                send_sem=send_sem.at[stage, i], recv_sem=recv_sem.at[stage, slot],
                device_id=peer, device_id_type=MESH,
            )
            for i, peer in enumerate(stage_peers[stage])
        ]

    tree_sends = []

    def tree_send(buffer, send_sem, recv_sem, stage):
        copies = tree_copies(buffer, send_sem, recv_sem, stage)
        for copy in copies:
            copy.start()
        tree_sends.extend(copies)

    def tree_wait(buffer, recv_sem, stage):
        for step in range(1, 8):
            slot = (place8[stage] + step) % 8
            pltpu.make_async_copy(
                buffer.at[stage, slot], buffer.at[stage, slot], recv_sem.at[stage, slot]
            ).wait()

    for copy in fetches[:4]:
        copy.wait()
    order = order_ref[...]
    pts = pts_ref[...].astype(BF16)
    own_aug = augment(pts.astype(F32), 0.0)
    own_std = jnp.concatenate([pts, own_aug.astype(BF16)], axis=0)
    skels = []
    for own in range(2):
        where = lookup(order[:, own * HALF : (own + 1) * HALF], lsk_ref[own : own + 1, :])
        skels.append(choose(own_std, where))
    pair = jnp.concatenate(skels, axis=1)
    node = choose(pair, psk_ref[...])
    tp[0, pl.ds(place8[0], 1)] = node[None, 0:DIM]

    group_entered()
    tree_send(tp, psend, precv, 0)

    second = order[:, HALF:]
    grid = lax.dot_general(
        onehot(second >> 7, 8), onehot(second & 127, 128), NT, preferred_element_type=F32
    )
    member = jnp.concatenate([grid[k : k + 1] for k in range(8)], axis=1)
    for copy in fetches[4:]:
        copy.wait()
    chg_hi, chg_lo = split2(chg_ref[...])
    row = lax.broadcasted_iota(jnp.int32, (AUG, PTS), 0)
    win[4, 0:DIM] = pts
    win[4, DIM:AUGD] = jnp.where(row == 3, member, own_aug).astype(BF16)
    win[4, AUGD:WROWS] = chg_hi

    def window_copy(slot, target_slot, index, peer):
        return pltpu.make_async_remote_copy(
            src_ref=win.at[slot], dst_ref=win.at[target_slot],
            send_sem=wsend.at[index], recv_sem=wrecv.at[target_slot],
            device_id=peer, device_id_type=MESH,
        )

    ours, theirs = 8 * core, 8 * (1 - core)
    sends = []

    def window_send(*args):
        sends.append(window_copy(*args))
        sends[-1].start()

    window_send(4, ours, 1, (partner, sub))

    def window_wait(slot):
        pltpu.make_async_copy(win.at[slot], win.at[slot], wrecv.at[slot]).wait()

    weights = []
    for own in range(2):
        mine = member if own else 1.0 - member
        masked = jnp.concatenate([chg_hi.astype(F32) * mine, chg_lo.astype(F32) * mine], axis=0)
        mat = gauss(own_std, swapped(skels[own])).astype(BF16)
        weights.append(stack2(apply_mat(masked.astype(BF16), mat)))
    pair_mat = gauss(pair, swapped(node)).astype(BF16)
    tu[0, pl.ds(place8[0], 1)] = stack2(
        apply_mat(jnp.concatenate(weights, axis=1), pair_mat)
    )[None]
    tree_send(tu, usend, urecv, 0)
    for step in (1, 3):
        window_send(4, 8 - step, 1 + step, x_peer(step))
    k = lax.broadcasted_iota(jnp.int32, (24, 32), 0)
    slot_k = k // 2
    ids = ((leaf + slot_k // 4 - 1) * 4 + (sub + slot_k % 4) % 4) * 2 + k % 2
    for own in range(2):
        hit = jnp.where(nbr_ref[own : own + 1, :] == ids, msk_ref[own : own + 1, :], 0)
        total = jnp.sum(hit.astype(F32), axis=1, keepdims=True)
        cnt[own] = jnp.broadcast_to(total, (24, 128))

    own_swp[...] = swapped(own_std)
    for own in range(2):
        leaf_mats[own, :, 0:PTS] = gauss(skels[own], own_swp[...]).astype(BF16)
        leaf_mats[own, :, PTS:] = gauss(node, swapped(skels[own])).astype(BF16)
        mat = gauss(skels[1 - own], swapped(skels[own])).astype(BF16)
        far[9 + own] = apply_mat(weights[1 - own], mat)

    acc[...] = jnp.zeros_like(acc)

    def near(slot):
        aug = win[slot, DIM:AUGD].astype(F32)
        group = aug[3:4]
        charge = win[slot, AUGD:WROWS].astype(F32)
        rows = []
        for own in range(2):
            c0 = cnt[own, pl.ds(2 * slot, 1), 0:1]
            c1 = cnt[own, pl.ds(2 * slot + 1, 1), 0:1]
            rows.append(charge * (c0 + (c1 - c0) * group))
        rows = jnp.concatenate(rows, axis=0).astype(BF16)
        mat = gauss(win[slot, 0:AUGD], own_swp[...]).astype(BF16)
        acc[...] += jnp.dot(rows, mat, preferred_element_type=F32)

    firsts = [(256, 128, 64), (32, 16, 8), (4, 2, 0)]
    bases = [device // 8, device // 64, 0 * device]

    def chosen_rows(stage, depth):
        count = 4 >> depth
        start = firsts[stage][depth] + bases[stage] * count
        return [usk_ref[pl.ds(start + j, 1), :] for j in range(count)]

    def compose(stage):
        at = [sel + 256 * j for j, sel in enumerate(chosen_rows(stage, 0))]
        for depth in (1, 2):
            at = [
                lookup(jnp.concatenate(at[2 * j : 2 * j + 2], axis=1), sel)
                for j, sel in enumerate(chosen_rows(stage, depth))
            ]
        tops[stage] = onehot(at[0], 8 * SKEL)

    def select_stage(stage):
        tree_wait(tp, precv, stage)
        raw = [tp[stage, j] for j in range(8)]
        if stage < 2:
            wide = jnp.concatenate(raw, axis=1)
            top = jnp.dot(wide, tops[stage], preferred_element_type=F32).astype(BF16)
            tp[stage + 1, pl.ds(place8[stage + 1], 1)] = top[None]
            tree_send(tp, psend, precv, stage + 1)
            if stage == 0:
                window_send(4, 6, 3, x_peer(2))
        nodes = []
        for j in range(8):
            rows = augment(raw[j].astype(F32), 0.0).astype(BF16)
            nodes.append(jnp.concatenate([raw[j], rows], axis=0))
            n8[stage, j] = nodes[-1]
        for depth, kept in ((0, n4), (1, n2)):
            sels = chosen_rows(stage, depth)
            nodes = [
                choose(jnp.concatenate(nodes[2 * j : 2 * j + 2], axis=1), sel)
                for j, sel in enumerate(sels)
            ]
            for j, found in enumerate(nodes):
                kept[stage, j] = found
        if stage < 2:
            return choose(jnp.concatenate(nodes, axis=1), chosen_rows(stage, 2)[0])
        return None

    def pair_of(buffer, stage, j):
        return jnp.concatenate([buffer[stage, 2 * j], buffer[stage, 2 * j + 1]], axis=1)

    def path_of(stage):
        a = place8[stage]
        b, c = a // 2, a // 4
        return (a, a + 1 - 2 * (a % 2)), (b, b + 1 - 2 * (b % 2)), (c, 1 - c)

    def matrices(stage, top):
        for j in range(4):
            ups[stage, j] = gauss(pair_of(n8, stage, j), swapped(n4[stage, j])).astype(BF16)
        for j in range(2):
            ups[stage, 4 + j] = gauss(pair_of(n4, stage, j), swapped(n2[stage, j])).astype(BF16)
        if top is not None:
            ups[stage, 6] = gauss(pair_of(n2, stage, 0), swapped(top)).astype(BF16)
        (a, a1), (b, b1), (c, c1) = path_of(stage)
        node8, node4, node2 = n8[stage, a], n4[stage, b], n2[stage, c]
        crosses[3 * stage] = gauss(n8[stage, a1], swapped(node8)).astype(BF16)
        crosses[3 * stage + 1] = gauss(n4[stage, b1], swapped(node4)).astype(BF16)
        crosses[3 * stage + 2] = gauss(n2[stage, c1], swapped(node2)).astype(BF16)
        downs[3 * stage] = gauss(node4, swapped(node8)).astype(BF16)
        downs[3 * stage + 1] = gauss(node2, swapped(node4)).astype(BF16)
        if top is not None:
            downs[3 * stage + 2] = gauss(top, swapped(node2)).astype(BF16)

    def weights_stage(stage):
        tree_wait(tu, urecv, stage)
        for j in range(4):
            u4[stage, j] = stack2(apply_mat(pair_of(tu, stage, j), ups[stage, j]))
        for j in range(2):
            u2[stage, j] = stack2(apply_mat(pair_of(u4, stage, j), ups[stage, 4 + j]))
        if stage < 2:
            top = stack2(apply_mat(pair_of(u2, stage, 0), ups[stage, 6]))
            tu[stage + 1, pl.ds(place8[stage + 1], 1)] = top[None]
            tree_send(tu, usend, urecv, stage + 1)
        (a, a1), (b, b1), (c, c1) = path_of(stage)
        far[3 * stage] = apply_mat(tu[stage, a1], crosses[3 * stage])
        far[3 * stage + 1] = apply_mat(u4[stage, b1], crosses[3 * stage + 1])
        far[3 * stage + 2] = apply_mat(u2[stage, c1], crosses[3 * stage + 2])

    def way_down():
        value = far[5]
        for index in range(4, -1, -1):
            value = far[index] + apply_mat(stack2(value), downs[index])
        mat = downs[5].astype(F32)
        for index in range(4, -1, -1):
            mat = apply_mat(stack2(mat), downs[index])
        mat = stack2(mat)
        for own in range(2):
            to_leaf, to_points = leaf_mats[own, :, PTS:], leaf_mats[own, :, 0:PTS]
            term = far[9 + own] + apply_mat(stack2(value), to_leaf)
            acc[own * RHS : (own + 1) * RHS] += apply_mat(stack2(term), to_points)
            upper[own] = apply_mat(stack2(apply_mat(mat, to_leaf)), to_points).astype(BF16)

    compose(0)
    compose(1)
    near(4)
    far_entered()
    window_send(4, theirs, 0, (beyond, sub))
    top = select_stage(0)
    window_wait(theirs)
    matrices(0, top)
    near(theirs)
    weights_stage(0)

    def group_block(i, carry):
        near(5 + 2 * i)
        return carry

    def beyond_block(i, carry):
        slot = ours + 1 + 2 * i
        window_wait(slot)
        near(slot)
        return carry

    for dx in (1, 3):
        window_wait(4 + dx)
        window_send(4 + dx, ours + dx, 7 + dx, (partner, sub))
    lax.fori_loop(0, 2, group_block, 0)
    window_wait(ours)
    for step in (1, 3):
        window_send(ours, ours + (4 - step), 4 + step // 2, x_peer(step))
    near(ours)
    top = select_stage(1)
    window_wait(6)
    window_send(6, theirs + 2, 6, (beyond, sub))
    window_send(6, ours + 2, 9, (partner, sub))
    matrices(1, top)
    near(6)
    weights_stage(1)
    for dx in (1, 3, 2):
        window_wait(theirs + dx)
    near(theirs + 1)
    near(theirs + 3)
    near(theirs + 2)
    way_down()
    lax.fori_loop(0, 2, beyond_block, 0)
    window_wait(ours + 2)
    near(ours + 2)
    select_stage(2)
    matrices(2, None)
    weights_stage(2)

    value = far[8]
    for index in (7, 6):
        value = far[index] + apply_mat(stack2(value), downs[index])
    stacked = stack2(value)
    for own in range(2):
        acc[own * RHS : (own + 1) * RHS] += apply_mat(stacked, upper[own])

    mine = win[4, DIM:AUGD].astype(F32)[3:4]
    out_ref[...] = jnp.where(mine > 0.5, acc[RHS:], acc[:RHS])

    for copy in sends + tree_sends:
        copy.wait_send()


def shards(points, charges, order, neighbours, neighbour_mask, leaf_skel, pair_skel, upper_skel):
    call = pl.pallas_call(
        functools.partial(body, 8, 8),
        out_shape=jax.ShapeDtypeStruct((RHS, PTS), F32),
        in_specs=[pl.BlockSpec(memory_space=pl.ANY)] * 8,
        out_specs=pl.BlockSpec(memory_space=pltpu.VMEM),
        scratch_shapes=[
            pltpu.VMEM((DIM, PTS), F32),
            pltpu.VMEM((RHS, PTS), F32),
            pltpu.VMEM(order.shape, jnp.int32),
            pltpu.VMEM(neighbours.shape, jnp.int32),
            pltpu.VMEM(neighbour_mask.shape, jnp.int32),
            pltpu.VMEM(leaf_skel.shape, jnp.int32),
            pltpu.VMEM(pair_skel.shape, jnp.int32),
            pltpu.VMEM(upper_skel.shape, jnp.int32),
            pltpu.SemaphoreType.DMA((8,)),
            pltpu.VMEM((12, WROWS, PTS), BF16),
            pltpu.VMEM((AUGD, PTS), BF16),
            pltpu.VMEM((2 * RHS, PTS), F32),
            pltpu.VMEM((2, 24, 128), F32),
            pltpu.VMEM((3, 8, DIM, SKEL), BF16),
            pltpu.VMEM((3, 8, UROWS, SKEL), BF16),
            pltpu.VMEM((3, 8, AUGD, SKEL), BF16),
            pltpu.VMEM((3, 4, AUGD, SKEL), BF16),
            pltpu.VMEM((3, 2, AUGD, SKEL), BF16),
            pltpu.VMEM((3, 4, UROWS, SKEL), BF16),
            pltpu.VMEM((3, 2, UROWS, SKEL), BF16),
            pltpu.VMEM((3, 7, 2 * SKEL, SKEL), BF16),
            pltpu.VMEM((9, SKEL, SKEL), BF16),
            pltpu.VMEM((8, SKEL, SKEL), BF16),
            pltpu.VMEM((11, RHS, SKEL), F32),
            pltpu.VMEM((2, SKEL, PTS + SKEL), BF16),
            pltpu.VMEM((2, 8 * SKEL, SKEL), BF16),
            pltpu.VMEM((2, SKEL, PTS), BF16),
            pltpu.SemaphoreType.DMA((11,)),
            pltpu.SemaphoreType.DMA((12,)),
            pltpu.SemaphoreType.DMA((3, 7)),
            pltpu.SemaphoreType.DMA((3, 8)),
            pltpu.SemaphoreType.DMA((3, 7)),
            pltpu.SemaphoreType.DMA((3, 8)),
            pltpu.SemaphoreType.REGULAR,
            pltpu.SemaphoreType.REGULAR,
        ],
        compiler_params=pltpu.CompilerParams(
            collective_id=0, has_side_effects=True, vmem_limit_bytes=56 << 20
        ),
        name="krr_matvec",
    )
    out = call(
        points.T, charges.T, order, neighbours, neighbour_mask, leaf_skel, pair_skel, upper_skel
    )
    return out.T


def solution(mesh):
    placed = (P(("leaf", "sub"), None),) * 7 + (P(),)
    return jax.shard_map(
        shards, mesh=mesh, in_specs=placed, out_specs=P(("leaf", "sub"), None), check_vma=False
    )
```

```python
import functools

import jax
import jax.numpy as jnp
from jax import lax
from jax.experimental import pallas as pl
from jax.experimental.pallas import tpu as pltpu
from jax.sharding import PartitionSpec as P

F32 = jnp.float32
BF16 = jnp.bfloat16
MESH = pl.DeviceIdType.MESH
TN = (((0,), (0,)), ((), ()))
NT = (((1,), (1,)), ((), ()))
LOG2E = 1.4426950408889634

DIM = 64
AUG = 16
RHS = 16
PTS = 1024
SKEL = 128
HALF = PTS // 2
AUGD = DIM + AUG
WROWS = AUGD + RHS
UROWS = 2 * RHS


def split2(value):
    high = value.astype(BF16)
    return high, (value - high.astype(F32)).astype(BF16)


def split3(value):
    high = value.astype(BF16)
    rest = value - high.astype(F32)
    mid = rest.astype(BF16)
    return high.astype(F32), mid.astype(F32), (rest - mid.astype(F32)).astype(BF16).astype(F32)


def augment(pts_f32, member):
    width = pts_f32.shape[1]
    n = -0.5 * jnp.sum(pts_f32 * pts_f32, axis=0, keepdims=True)
    hi, mid, lo = split3(n)
    row = lax.broadcasted_iota(jnp.int32, (AUG, width), 0)
    out = jnp.where(row == 0, hi, jnp.where(row == 1, mid, jnp.where(row == 2, lo, 0.0)))
    out = jnp.where(row == 3, member, out)
    return jnp.where((row >= 8) & (row < 11), 1.0, out)


def swapped(block):
    aug = block[DIM:AUGD].astype(F32)
    aug = jnp.concatenate([aug[8:], aug[:8]], axis=0).astype(BF16)
    return jnp.concatenate([block[:DIM], aug], axis=0)


def gauss(std, swp):
    scale = LOG2E * 4.0 / DIM
    inner = lax.dot_general(std, swp, TN, preferred_element_type=F32)
    return jnp.exp2(inner * scale)


def stack2(value):
    high, low = split2(value)
    return jnp.concatenate([high, low], axis=0)


def apply_mat(stacked, mat):
    both = jnp.dot(stacked, mat, preferred_element_type=F32)
    half = both.shape[0] // 2
    return both[:half] + both[half:]


def onehot(sel, rows):
    at = lax.broadcasted_iota(jnp.int32, (rows, sel.shape[1]), 0)
    return jnp.where(at == sel, 1.0, 0.0).astype(BF16)


def choose(points, sel):
    return jnp.dot(points, onehot(sel, points.shape[1]), preferred_element_type=F32).astype(BF16)


def lookup(table, sel):
    pad = jnp.zeros((6, table.shape[1]), F32)
    rows = jnp.concatenate([(table >> 5).astype(F32), (table & 31).astype(F32), pad], axis=0)
    found = jnp.dot(rows.astype(BF16), onehot(sel, table.shape[1]), preferred_element_type=F32)
    return (found[0:1] * 32.0 + found[1:2]).astype(jnp.int32)


def body(
    y_size, z_size,
    pts_in, chg_in, order_in, nbr_in, msk_in, lsk_in, psk_in, usk_in,
    out_ref,
    pts_ref, chg_ref, order_ref, nbr_ref, msk_ref, lsk_ref, psk_ref, usk_ref, fetched,
    win, own_swp, acc, cnt, tp, tu, n8, n4, n2, u4, u2, ups, crosses, downs, far, leaf_mats, tops, upper,
    wsend, wrecv, psend, precv, usend, urecv, near_in, far_in,
):
    leaf = lax.axis_index("leaf")
    sub = lax.axis_index("sub")
    leaf_count = lax.axis_size("leaf")
    device = leaf * 4 + sub
    core = leaf % 2
    z = (leaf // 2) % z_size
    y = leaf // (2 * z_size)
    partner = leaf + 1 - 2 * core

    def x_peer(step):
        return (leaf, (sub + step) % 4)

    def z_peer(step):
        return ((y * z_size + (z + step) % z_size) * 2 + core, sub)

    def y_peer(step):
        return ((((y + step) % y_size) * z_size + z) * 2 + core, sub)

    other_core = [(partner, (sub + step) % 4) for step in (0, 1, 3, 2)]
    beyond = (leaf + leaf_count - 1 + 2 * core) % leaf_count
    stage_peers = [
        [x_peer(s) for s in (2, 1, 3)] + other_core,
        [z_peer(s) for s in (4, 3, 5, 2, 6, 1, 7)],
        [y_peer(s) for s in (4, 3, 5, 2, 6, 1, 7)],
    ]
    barrier = pltpu.get_barrier_semaphore()
    own_chip = (leaf - core, leaf - core + 1)

    def signal(semaphore, peer):
        pl.semaphore_signal(semaphore, inc=1, device_id=peer, device_id_type=MESH)

    for step in (1, 2, 3):
        signal(barrier, (own_chip[0], (sub + step) % 4))

    @pl.when(core == 1)
    def _():
        signal(barrier, (own_chip[0], sub))

    for step in range(1, 8):
        signal(barrier, ((y * z_size + (z + step) % z_size) * 2 + 1, sub))
        signal(barrier, ((((y + step) % y_size) * z_size + z) * 2 + 1, sub))
    signal(barrier, (beyond - beyond % 2 + 1, sub))

    fetches = [
        pltpu.make_async_copy(source, target, fetched.at[i])
        for i, (source, target) in enumerate(
            (
                (order_in, order_ref), (lsk_in, lsk_ref), (psk_in, psk_ref), (pts_in, pts_ref),
                (chg_in, chg_ref), (nbr_in, nbr_ref), (msk_in, msk_ref), (usk_in, usk_ref),
            )
        )
    ]
    for copy in fetches:
        copy.start()

    def group_entered():
        @pl.when(core == 0)
        def _():
            pl.semaphore_wait(barrier, 7)
            signal(near_in, (own_chip[1], sub))

        @pl.when(core == 1)
        def _():
            pl.semaphore_wait(near_in, 1)

    def far_entered():
        @pl.when(core == 1)
        def _():
            pl.semaphore_wait(barrier, 2 * (z_size - 1) + 2 * (y_size - 1) + 2)
            signal(far_in, (own_chip[0], sub))

        @pl.when(core == 0)
        def _():
            pl.semaphore_wait(far_in, 1)

    place8 = [core * 4 + sub, z, y]

    def tree_copies(buffer, send_sem, recv_sem, stage):
        slot = place8[stage]
        return [
            pltpu.make_async_remote_copy(
                src_ref=buffer.at[stage, slot], dst_ref=buffer.at[stage, slot],
                send_sem=send_sem.at[stage, i], recv_sem=recv_sem.at[stage, slot],
                device_id=peer, device_id_type=MESH,
            )
            for i, peer in enumerate(stage_peers[stage])
        ]

    tree_sends = []

    def tree_send(buffer, send_sem, recv_sem, stage):
        copies = tree_copies(buffer, send_sem, recv_sem, stage)
        for copy in copies:
            copy.start()
        tree_sends.extend(copies)

    def tree_wait(buffer, recv_sem, stage):
        for step in range(1, 8):
            slot = (place8[stage] + step) % 8
            pltpu.make_async_copy(
                buffer.at[stage, slot], buffer.at[stage, slot], recv_sem.at[stage, slot]
            ).wait()

    for copy in fetches[:4]:
        copy.wait()
    order = order_ref[...]
    pts = pts_ref[...].astype(BF16)
    own_aug = augment(pts.astype(F32), 0.0)
    own_std = jnp.concatenate([pts, own_aug.astype(BF16)], axis=0)
    skels = []
    for own in range(2):
        where = lookup(order[:, own * HALF : (own + 1) * HALF], lsk_ref[own : own + 1, :])
        skels.append(choose(own_std, where))
    pair = jnp.concatenate(skels, axis=1)
    node = choose(pair, psk_ref[...])
    tp[0, pl.ds(place8[0], 1)] = node[None, 0:DIM]

    group_entered()
    tree_send(tp, psend, precv, 0)

    second = order[:, HALF:]
    grid = lax.dot_general(
        onehot(second >> 7, 8), onehot(second & 127, 128), NT, preferred_element_type=F32
    )
    member = jnp.concatenate([grid[k : k + 1] for k in range(8)], axis=1)
    for copy in fetches[4:]:
        copy.wait()
    chg_hi, chg_lo = split2(chg_ref[...])
    row = lax.broadcasted_iota(jnp.int32, (AUG, PTS), 0)
    win[4, 0:DIM] = pts
    win[4, DIM:AUGD] = jnp.where(row == 3, member, own_aug).astype(BF16)
    win[4, AUGD:WROWS] = chg_hi

    def window_copy(slot, target_slot, index, peer):
        return pltpu.make_async_remote_copy(
            src_ref=win.at[slot], dst_ref=win.at[target_slot],
            send_sem=wsend.at[index], recv_sem=wrecv.at[target_slot],
            device_id=peer, device_id_type=MESH,
        )

    ours, theirs = 8 * core, 8 * (1 - core)
    sends = []

    def window_send(*args):
        sends.append(window_copy(*args))
        sends[-1].start()

    window_send(4, ours, 1, (partner, sub))

    def window_wait(slot):
        pltpu.make_async_copy(win.at[slot], win.at[slot], wrecv.at[slot]).wait()

    weights = []
    for own in range(2):
        mine = member if own else 1.0 - member
        masked = jnp.concatenate([chg_hi.astype(F32) * mine, chg_lo.astype(F32) * mine], axis=0)
        mat = gauss(own_std, swapped(skels[own])).astype(BF16)
        weights.append(stack2(apply_mat(masked.astype(BF16), mat)))
    pair_mat = gauss(pair, swapped(node)).astype(BF16)
    tu[0, pl.ds(place8[0], 1)] = stack2(
        apply_mat(jnp.concatenate(weights, axis=1), pair_mat)
    )[None]
    tree_send(tu, usend, urecv, 0)
    for step in (1, 3):
        window_send(4, 8 - step, 1 + step, x_peer(step))
    k = lax.broadcasted_iota(jnp.int32, (24, 32), 0)
    slot_k = k // 2
    ids = ((leaf + slot_k // 4 - 1) * 4 + (sub + slot_k % 4) % 4) * 2 + k % 2
    for own in range(2):
        hit = jnp.where(nbr_ref[own : own + 1, :] == ids, msk_ref[own : own + 1, :], 0)
        total = jnp.sum(hit.astype(F32), axis=1, keepdims=True)
        cnt[own] = jnp.broadcast_to(total, (24, 128))

    own_swp[...] = swapped(own_std)
    for own in range(2):
        leaf_mats[own, :, 0:PTS] = gauss(skels[own], own_swp[...]).astype(BF16)
        leaf_mats[own, :, PTS:] = gauss(node, swapped(skels[own])).astype(BF16)
        mat = gauss(skels[1 - own], swapped(skels[own])).astype(BF16)
        far[9 + own] = apply_mat(weights[1 - own], mat)

    acc[...] = jnp.zeros_like(acc)

    def near(slot):
        aug = win[slot, DIM:AUGD].astype(F32)
        group = aug[3:4]
        charge = win[slot, AUGD:WROWS].astype(F32)
        rows = []
        for own in range(2):
            c0 = cnt[own, pl.ds(2 * slot, 1), 0:1]
            c1 = cnt[own, pl.ds(2 * slot + 1, 1), 0:1]
            rows.append(charge * (c0 + (c1 - c0) * group))
        rows = jnp.concatenate(rows, axis=0).astype(BF16)
        mat = gauss(win[slot, 0:AUGD], own_swp[...]).astype(BF16)
        acc[...] += jnp.dot(rows, mat, preferred_element_type=F32)

    firsts = [(256, 128, 64), (32, 16, 8), (4, 2, 0)]
    bases = [device // 8, device // 64, 0 * device]

    def chosen_rows(stage, depth):
        count = 4 >> depth
        start = firsts[stage][depth] + bases[stage] * count
        return [usk_ref[pl.ds(start + j, 1), :] for j in range(count)]

    def compose(stage):
        at = [sel + 256 * j for j, sel in enumerate(chosen_rows(stage, 0))]
        for depth in (1, 2):
            at = [
                lookup(jnp.concatenate(at[2 * j : 2 * j + 2], axis=1), sel)
                for j, sel in enumerate(chosen_rows(stage, depth))
            ]
        tops[stage] = onehot(at[0], 8 * SKEL)

    def select_stage(stage):
        tree_wait(tp, precv, stage)
        raw = [tp[stage, j] for j in range(8)]
        if stage < 2:
            wide = jnp.concatenate(raw, axis=1)
            top = jnp.dot(wide, tops[stage], preferred_element_type=F32).astype(BF16)
            tp[stage + 1, pl.ds(place8[stage + 1], 1)] = top[None]
            tree_send(tp, psend, precv, stage + 1)
            if stage == 0:
                window_send(4, 6, 3, x_peer(2))
        nodes = []
        for j in range(8):
            rows = augment(raw[j].astype(F32), 0.0).astype(BF16)
            nodes.append(jnp.concatenate([raw[j], rows], axis=0))
            n8[stage, j] = nodes[-1]
        for depth, kept in ((0, n4), (1, n2)):
            sels = chosen_rows(stage, depth)
            nodes = [
                choose(jnp.concatenate(nodes[2 * j : 2 * j + 2], axis=1), sel)
                for j, sel in enumerate(sels)
            ]
            for j, found in enumerate(nodes):
                kept[stage, j] = found
        if stage < 2:
            return choose(jnp.concatenate(nodes, axis=1), chosen_rows(stage, 2)[0])
        return None

    def pair_of(buffer, stage, j):
        return jnp.concatenate([buffer[stage, 2 * j], buffer[stage, 2 * j + 1]], axis=1)

    def path_of(stage):
        a = place8[stage]
        b, c = a // 2, a // 4
        return (a, a + 1 - 2 * (a % 2)), (b, b + 1 - 2 * (b % 2)), (c, 1 - c)

    def matrices(stage, top):
        for j in range(4):
            ups[stage, j] = gauss(pair_of(n8, stage, j), swapped(n4[stage, j])).astype(BF16)
        for j in range(2):
            ups[stage, 4 + j] = gauss(pair_of(n4, stage, j), swapped(n2[stage, j])).astype(BF16)
        if top is not None:
            ups[stage, 6] = gauss(pair_of(n2, stage, 0), swapped(top)).astype(BF16)
        (a, a1), (b, b1), (c, c1) = path_of(stage)
        node8, node4, node2 = n8[stage, a], n4[stage, b], n2[stage, c]
        crosses[3 * stage] = gauss(n8[stage, a1], swapped(node8)).astype(BF16)
        crosses[3 * stage + 1] = gauss(n4[stage, b1], swapped(node4)).astype(BF16)
        crosses[3 * stage + 2] = gauss(n2[stage, c1], swapped(node2)).astype(BF16)
        downs[3 * stage] = gauss(node4, swapped(node8)).astype(BF16)
        downs[3 * stage + 1] = gauss(node2, swapped(node4)).astype(BF16)
        if top is not None:
            downs[3 * stage + 2] = gauss(top, swapped(node2)).astype(BF16)

    def weights_stage(stage):
        tree_wait(tu, urecv, stage)
        for j in range(4):
            u4[stage, j] = stack2(apply_mat(pair_of(tu, stage, j), ups[stage, j]))
        for j in range(2):
            u2[stage, j] = stack2(apply_mat(pair_of(u4, stage, j), ups[stage, 4 + j]))
        if stage < 2:
            top = stack2(apply_mat(pair_of(u2, stage, 0), ups[stage, 6]))
            tu[stage + 1, pl.ds(place8[stage + 1], 1)] = top[None]
            tree_send(tu, usend, urecv, stage + 1)
        (a, a1), (b, b1), (c, c1) = path_of(stage)
        far[3 * stage] = apply_mat(tu[stage, a1], crosses[3 * stage])
        far[3 * stage + 1] = apply_mat(u4[stage, b1], crosses[3 * stage + 1])
        far[3 * stage + 2] = apply_mat(u2[stage, c1], crosses[3 * stage + 2])

    def way_down():
        value = far[5]
        for index in range(4, -1, -1):
            value = far[index] + apply_mat(stack2(value), downs[index])
        mat = downs[5].astype(F32)
        for index in range(4, -1, -1):
            mat = apply_mat(stack2(mat), downs[index])
        mat = stack2(mat)
        for own in range(2):
            to_leaf, to_points = leaf_mats[own, :, PTS:], leaf_mats[own, :, 0:PTS]
            term = far[9 + own] + apply_mat(stack2(value), to_leaf)
            acc[own * RHS : (own + 1) * RHS] += apply_mat(stack2(term), to_points)
            upper[own] = apply_mat(stack2(apply_mat(mat, to_leaf)), to_points).astype(BF16)

    compose(0)
    compose(1)
    near(4)
    far_entered()
    window_send(4, theirs, 0, (beyond, sub))
    top = select_stage(0)
    matrices(0, top)
    weights_stage(0)
    window_wait(theirs)
    near(theirs)

    def group_block(i, carry):
        near(5 + 2 * i)
        return carry

    def beyond_block(i, carry):
        slot = ours + 1 + 2 * i
        window_wait(slot)
        near(slot)
        return carry

    for dx in (1, 3):
        window_wait(4 + dx)
        window_send(4 + dx, ours + dx, 7 + dx, (partner, sub))
    lax.fori_loop(0, 2, group_block, 0)
    window_wait(ours)
    for step in (1, 3):
        window_send(ours, ours + (4 - step), 7 - 2 * (step // 2), x_peer(step))
    near(ours)
    top = select_stage(1)
    matrices(1, top)
    weights_stage(1)
    window_wait(6)
    window_send(6, theirs + 2, 6, (beyond, sub))
    window_send(6, ours + 2, 9, (partner, sub))
    near(6)
    for dx in (1, 3, 2):
        window_wait(theirs + dx)
    near(theirs + 1)
    near(theirs + 3)
    near(theirs + 2)
    way_down()
    lax.fori_loop(0, 2, beyond_block, 0)
    window_wait(ours + 2)
    near(ours + 2)
    select_stage(2)
    matrices(2, None)
    weights_stage(2)

    value = far[8]
    for index in (7, 6):
        value = far[index] + apply_mat(stack2(value), downs[index])
    stacked = stack2(value)
    for own in range(2):
        acc[own * RHS : (own + 1) * RHS] += apply_mat(stacked, upper[own])

    mine = win[4, DIM:AUGD].astype(F32)[3:4]
    out_ref[...] = jnp.where(mine > 0.5, acc[RHS:], acc[:RHS])

    for copy in sends + tree_sends:
        copy.wait_send()


def shards(points, charges, order, neighbours, neighbour_mask, leaf_skel, pair_skel, upper_skel):
    call = pl.pallas_call(
        functools.partial(body, 8, 8),
        out_shape=jax.ShapeDtypeStruct((RHS, PTS), F32),
        in_specs=[pl.BlockSpec(memory_space=pl.ANY)] * 8,
        out_specs=pl.BlockSpec(memory_space=pltpu.VMEM),
        scratch_shapes=[
            pltpu.VMEM((DIM, PTS), F32),
            pltpu.VMEM((RHS, PTS), F32),
            pltpu.VMEM(order.shape, jnp.int32),
            pltpu.VMEM(neighbours.shape, jnp.int32),
            pltpu.VMEM(neighbour_mask.shape, jnp.int32),
            pltpu.VMEM(leaf_skel.shape, jnp.int32),
            pltpu.VMEM(pair_skel.shape, jnp.int32),
            pltpu.VMEM(upper_skel.shape, jnp.int32),
            pltpu.SemaphoreType.DMA((8,)),
            pltpu.VMEM((12, WROWS, PTS), BF16),
            pltpu.VMEM((AUGD, PTS), BF16),
            pltpu.VMEM((2 * RHS, PTS), F32),
            pltpu.VMEM((2, 24, 128), F32),
            pltpu.VMEM((3, 8, DIM, SKEL), BF16),
            pltpu.VMEM((3, 8, UROWS, SKEL), BF16),
            pltpu.VMEM((3, 8, AUGD, SKEL), BF16),
            pltpu.VMEM((3, 4, AUGD, SKEL), BF16),
            pltpu.VMEM((3, 2, AUGD, SKEL), BF16),
            pltpu.VMEM((3, 4, UROWS, SKEL), BF16),
            pltpu.VMEM((3, 2, UROWS, SKEL), BF16),
            pltpu.VMEM((3, 7, 2 * SKEL, SKEL), BF16),
            pltpu.VMEM((9, SKEL, SKEL), BF16),
            pltpu.VMEM((8, SKEL, SKEL), BF16),
            pltpu.VMEM((11, RHS, SKEL), F32),
            pltpu.VMEM((2, SKEL, PTS + SKEL), BF16),
            pltpu.VMEM((2, 8 * SKEL, SKEL), BF16),
            pltpu.VMEM((2, SKEL, PTS), BF16),
            pltpu.SemaphoreType.DMA((11,)),
            pltpu.SemaphoreType.DMA((12,)),
            pltpu.SemaphoreType.DMA((3, 7)),
            pltpu.SemaphoreType.DMA((3, 8)),
            pltpu.SemaphoreType.DMA((3, 7)),
            pltpu.SemaphoreType.DMA((3, 8)),
            pltpu.SemaphoreType.REGULAR,
            pltpu.SemaphoreType.REGULAR,
        ],
        compiler_params=pltpu.CompilerParams(
            collective_id=0, has_side_effects=True, vmem_limit_bytes=56 << 20
        ),
        name="krr_matvec",
    )
    out = call(
        points.T, charges.T, order, neighbours, neighbour_mask, leaf_skel, pair_skel, upper_skel
    )
    return out.T


def solution(mesh):
    placed = (P(("leaf", "sub"), None),) * 7 + (P(),)
    return jax.shard_map(
        shards, mesh=mesh, in_specs=placed, out_specs=P(("leaf", "sub"), None), check_vma=False
    )
```
